256 devices in a mesh: sub: 64 (over z_hi, x, y), freq: 4 (over z_lo, core).
Axes of the slice: x: 4, y: 4, z: 8 (z_hi: 4, z_lo: 2; z = z_hi * 2 + z_lo), core: 2. Of those that a mesh axis runs over, the one named last changes fastest.
Arguments:
- source: float32 [64, 2, 3, 32, 32, 128], P('sub'), may hold values from -6 to 6
- adjoint_source: float32 [4, 64, 2, 3, 32, 32, 128], P('freq', 'sub'), may hold values from -6 to 6
- sigma_h: float32 [64, 32, 32, 128], P('sub'), may hold values from 0.3 to 3
- sigma_v: float32 [64, 32, 32, 128], P('sub'), may hold values from 0.1 to 1
- seafloor: int32 [64, 32, 32], P('sub'), may hold values from 0 to 63
- links: int32 [64, 4], P('sub'), may hold values from 0 to 1, as said below
- freq_index: int32 [4], P('freq'), may hold values from 0 to 3, each once
Outputs:
- forward_field: float32 [4, 64, 2, 3, 32, 32, 128], P('freq', 'sub')
- grad_h: float32 [64, 32, 32, 128], P('sub')
- grad_v: float32 [64, 32, 32, 128], P('sub')
The draws below stay inside these ranges and needn't reach their ends.
Inputs may be any that keep to these rules, and one draw needn't show every extreme that they name: links is symmetric between lateral neighbours (the high x face of subdomain i and the low x face of subdomain i + 1, the high y face of i and the low y face of i + 8) and zero on the slab's outer faces.
All inputs are finite; a program needn't handle non-finite values.
Results may differ from the reference program's by a relative error of at most 0.0001.
Values sent between devices are 32-bit elements; how exact they have to be, the bound alone decides.
No kernel may reach another device: no remote copies, remote signals or barrier semaphores. Data moves between devices by JAX's collectives and lax.ppermute only.
A program may use at most 64 MiB of HBM per device.

```python
import math
import jax
import jax.numpy as jnp
from jax import lax

SX = 8
SY = 8
SUBS = 64
NFREQ = 4
CX = 32
CY = 32
CZ = 128
ITERS = 2


def draw_links(key, part):
    key = jax.random.fold_in(key, 7)
    key_x, key_y = jax.random.split(key)
    open_x = jax.random.randint(key_x, (SY, SX - 1), 0, 2).astype(jnp.int32)
    open_x = open_x.at[0, 0].set(1)
    open_y = jax.random.randint(key_y, (SY - 1, SX), 0, 2).astype(jnp.int32)
    edge_col = jnp.zeros((SY, 1), jnp.int32)
    edge_row = jnp.zeros((1, SX), jnp.int32)
    low_x = jnp.concatenate([edge_col, open_x], axis=1)
    high_x = jnp.concatenate([open_x, edge_col], axis=1)
    low_y = jnp.concatenate([edge_row, open_y], axis=0)
    high_y = jnp.concatenate([open_y, edge_row], axis=0)
    return jnp.stack([low_x, high_x, low_y, high_y], axis=-1).reshape(SUBS, 4)


def set_ends(values, stream_key, low, top_value):
    extent = values.shape
    index_at = [jax.random.randint(jax.random.fold_in(stream_key, axis), (), 0, extent[axis]) for axis in range(len(extent))]
    values = values.at[tuple(index_at)].set(low)
    longest = extent.index(max(extent))
    index_at[longest] = (index_at[longest] + 1) % extent[longest]
    return values.at[tuple(index_at)].set(top_value)


def level_of(stream_key, shape, cuts, least, high):
    def one(axis_at, shards_of):
        steps = jax.random.uniform(jax.random.fold_in(jax.random.fold_in(stream_key, 6), axis_at), (shards_of,), jnp.float32, least / len(cuts), high / len(cuts))
        return jnp.repeat(jnp.exp(steps), shape[axis_at] // shards_of).reshape((-1,) + (1,) * (len(shape) - axis_at - 1))

    loudness = one(*cuts[0])
    for cut in cuts[1:]:
        loudness = loudness * one(*cut)
    return loudness


def normal_values(stream_key, extent, width, bound, cuts=(), kind=jnp.bfloat16):
    loudness = level_of(stream_key, extent, cuts, -0.22, 0.18) if cuts else 1.0
    drawn = jax.random.normal(stream_key, extent, jnp.float32) * width * loudness
    return jnp.minimum(jnp.maximum(drawn, -bound), bound).astype(kind)


def setup_inputs(seed: int = 0) -> dict:
    streams_of = jax.random.split(jax.random.key(seed), 8)
    source = normal_values(streams_of[0], (SUBS, 2, 3, CX, CY, CZ), 1.0, 6.0, ((0, 64),), jnp.float32)
    adjoint_source = normal_values(streams_of[1], (NFREQ, SUBS, 2, 3, CX, CY, CZ), 1.0, 6.0, ((0, 4), (1, 64)), jnp.float32)
    sigma_h = jnp.clip(jnp.exp(math.log(3.0) - 2.3025851 * jax.random.uniform(streams_of[2], (SUBS, CX, CY, CZ), jnp.float32) ** level_of(streams_of[2], (SUBS, CX, CY, CZ), ((0, 64),), -0.2, 0.2)), 0.3, 3.0)
    sigma_v = jnp.clip(jnp.exp(math.log(1.0) - 2.3025851 * jax.random.uniform(streams_of[3], (SUBS, CX, CY, CZ), jnp.float32) ** level_of(streams_of[3], (SUBS, CX, CY, CZ), ((0, 64),), -0.2, 0.2)), 0.1, 1.0)
    seafloor = set_ends(jax.random.randint(streams_of[4], (SUBS, CX, CY), 0, CZ // 2), jax.random.fold_in(streams_of[4], 1), 0, (CZ // 2) - 1).astype(jnp.int32)
    links = draw_links(jax.random.fold_in(streams_of[7], 71), 0)
    freq_index = jax.random.permutation(streams_of[6], NFREQ).astype(jnp.int32)
    return {"source": source, "adjoint_source": adjoint_source, "sigma_h": sigma_h, "sigma_v": sigma_v, "seafloor": seafloor, "links": links, "freq_index": freq_index}


P_ROBIN = 0.25
OMEGA0 = 0.5


def update(rhs, shift3, mask):
    real_part = rhs[..., 0, :, :, :, :]
    imag_part = rhs[..., 1, :, :, :, :]
    denom = 36.0 + shift3 * shift3
    new_real = (6.0 * real_part + shift3 * imag_part) / denom
    new_imag = (6.0 * imag_part - shift3 * real_part) / denom
    return jnp.stack([new_real, new_imag], axis=-5) * mask[..., None, None, :, :, :]


def face_traces(field):
    low_x = (1.0 + P_ROBIN) * field[..., 0, :, :] - P_ROBIN * field[..., 1, :, :]
    high_x = (1.0 + P_ROBIN) * field[..., -1, :, :] - P_ROBIN * field[..., -2, :, :]
    low_y = (1.0 + P_ROBIN) * field[..., :, 0, :] - P_ROBIN * field[..., :, 1, :]
    high_y = (1.0 + P_ROBIN) * field[..., :, -1, :] - P_ROBIN * field[..., :, -2, :]
    return low_x, high_x, low_y, high_y


def stencil_sum(field, ghost_lo_x, ghost_hi_x, ghost_lo_y, ghost_hi_y):
    along_x = jnp.concatenate([ghost_lo_x[..., None, :, :], field, ghost_hi_x[..., None, :, :]], axis=-3)
    total = along_x[..., :-2, :, :] + along_x[..., 2:, :, :]
    along_y = jnp.concatenate([ghost_lo_y[..., :, None, :], field, ghost_hi_y[..., :, None, :]], axis=-2)
    total = total + along_y[..., :, :-2, :] + along_y[..., :, 2:, :]
    zero_plane = jnp.zeros_like(field[..., :1])
    along_z = jnp.concatenate([zero_plane, field, zero_plane], axis=-1)
    return total + along_z[..., :-2] + along_z[..., 2:]


def grid_ghosts(field, link_grid):
    low_x, high_x, low_y, high_y = face_traces(field)

    def flag(k):
        return link_grid[:, :, k][:, :, None, None, None, None]

    ghost_hi_x = jnp.concatenate([low_x[:, 1:], jnp.zeros_like(low_x[:, :1])], axis=1) * flag(1)
    ghost_lo_x = jnp.concatenate([jnp.zeros_like(high_x[:, :1]), high_x[:, :-1]], axis=1) * flag(0)
    ghost_hi_y = jnp.concatenate([low_y[1:], jnp.zeros_like(low_y[:1])], axis=0) * flag(3)
    ghost_lo_y = jnp.concatenate([jnp.zeros_like(high_y[:1]), high_y[:-1]], axis=0) * flag(2)
    return ghost_lo_x, ghost_hi_x, ghost_lo_y, ghost_hi_y


def solve_grid(source_grid, shift3, mask, link_grid):
    field = update(source_grid, shift3, mask)
    for sweep in range(ITERS):
        ghosts = grid_ghosts(field, link_grid)
        field = update(source_grid + stencil_sum(field, *ghosts), shift3, mask)
    return field


def reference(source, adjoint_source, sigma_h, sigma_v, seafloor, links, freq_index):
    depth = lax.broadcasted_iota(jnp.int32, (SUBS, CX, CY, CZ), 3)
    mask = (depth >= seafloor[..., None]).astype(jnp.float32).reshape(SY, SX, CX, CY, CZ)
    link_grid = links.astype(jnp.float32).reshape(SY, SX, 4)
    sh = sigma_h.reshape(SY, SX, CX, CY, CZ)
    sv = sigma_v.reshape(SY, SX, CX, CY, CZ)
    source_grid = source.reshape(SY, SX, 2, 3, CX, CY, CZ)
    total_h = jnp.zeros((SY, SX, CX, CY, CZ), jnp.float32)
    total_v = jnp.zeros((SY, SX, CX, CY, CZ), jnp.float32)
    fields = []
    for freq in range(NFREQ):
        scale = OMEGA0 * jnp.exp2(freq_index[freq].astype(jnp.float32))
        shift3 = scale * jnp.stack([sh, sh, sv], axis=-4)
        forward = solve_grid(source_grid, shift3, mask, link_grid)
        adjoint_grid = adjoint_source[freq].reshape(SY, SX, 2, 3, CX, CY, CZ)
        adjoint = solve_grid(adjoint_grid, shift3, mask, link_grid)
        product = adjoint[:, :, 0] * forward[:, :, 1] + adjoint[:, :, 1] * forward[:, :, 0]
        total_h = total_h + scale * (product[:, :, 0] + product[:, :, 1])
        total_v = total_v + scale * product[:, :, 2]
        fields.append(forward.reshape(SUBS, 2, 3, CX, CY, CZ))
    grad_h = (sh * mask * total_h).reshape(SUBS, CX, CY, CZ)
    grad_v = (sv * mask * total_v).reshape(SUBS, CX, CY, CZ)
    return jnp.stack(fields, axis=0), grad_h, grad_v
```

```python
import jax
import jax.numpy as jnp
from jax import lax
from jax.experimental import pallas as pl
from jax.experimental.pallas import tpu as pltpu
from jax.sharding import PartitionSpec as P

SX = 8
SUBS = 64
N = 32
NZ = 128
PLANE = 40
ROWS = 34 * PLANE
STEP = 8
BLOCK = STEP * N
CELLS = N * N
NF = 12
FACE = NF * N
X_V, X_S, X_R, X_C, X_ROWS = FACE, 2 * FACE, 2 * FACE + 64, 2 * FACE + 112, 2 * FACE + 120
Y_ROWS = 2 * FACE + 64
T_ROWS = 72

P_ROBIN = 0.25
OMEGA0 = 0.5
KEEP = 1.0 + P_ROBIN
f32 = jnp.float32


def whole(space=pltpu.VMEM):
    return pl.BlockSpec(memory_space=space)


def params(steps=0):
    kind = {"dimension_semantics": ("arbitrary",)} if steps else {}
    return pltpu.CompilerParams(vmem_limit_bytes=30 * 2**20, **kind)


def cost(flops, size):
    return pl.CostEstimate(flops=flops, bytes_accessed=size, transcendentals=0)


def base(x):
    return (x + 1) * PLANE


def scale_of(freq_ref):
    return OMEGA0 * jnp.left_shift(jnp.int32(1), freq_ref[0]).astype(f32)


def lane_neighbours(u):
    lane = lax.broadcasted_iota(jnp.int32, u.shape, 1)
    before = jnp.where(lane == 0, 0.0, pltpu.roll(u, 1, 1))
    after = jnp.where(lane == NZ - 1, 0.0, pltpu.roll(u, NZ - 1, 1))
    return before + after


def row_neighbours(u):
    row = lax.broadcasted_iota(jnp.int32, u.shape, 0)
    before = jnp.where(row == 0, 0.0, pltpu.roll(u, 1, 0))
    after = jnp.where(row == N - 1, 0.0, pltpu.roll(u, N - 1, 0))
    return before + after


def factors(shift):
    inverse = 1.0 / (36.0 + shift * shift)
    return jnp.where(shift > 0.0, 6.0 * inverse, 0.0), shift * inverse


def times(ab, re, im):
    a, b = ab
    return a * re + b * im, a * im - b * re


def pairs():
    for solve in range(2):
        for comp in range(3):
            yield solve * 6 + comp, solve * 6 + 3 + comp, comp // 2


def trace(outer, inner):
    return KEEP * outer - P_ROBIN * inner


def stencil(ref, f, x):
    start = base(x)
    centre = ref[f, pl.ds(start, N), :]
    total = ref[f, pl.ds(start - PLANE, N), :] + ref[f, pl.ds(start + PLANE, N), :]
    total = total + (ref[f, pl.ds(start - 1, N), :] + ref[f, pl.ds(start + 1, N), :])
    return total + lane_neighbours(centre)


def first_kernel(
    freq_ref, links_ref, floor_ref, src_ref, adj_ref, sh_ref, sv_ref,
    u_ref, v_ref, ab_ref, px0_ref, px1_ref, py0_ref, py1_ref,
    shift_ref, xl_ref, xh_ref, yl_ref, yh_ref,
):
    step = pl.program_id(0)
    scale = scale_of(freq_ref)

    @pl.when(step == 0)
    def _():
        zeros = jnp.zeros((PLANE, NZ), f32)
        for f in range(NF):
            for ref in (u_ref, v_ref):
                ref[f, 0:PLANE, :] = zeros
                ref[f, ROWS - PLANE:ROWS, :] = zeros

    @pl.when(step < N // STEP)
    def _():
        def plane(j, carry):
            x = step * STEP + j
            here = pl.ds(pl.multiple_of(j * N, N), N)
            there = pl.ds(pl.multiple_of(x * N, N), N)
            start = pl.multiple_of(base(x), 8)
            floor = floor_ref[pl.ds(x, 1), :].astype(f32)
            row = lax.broadcasted_iota(jnp.int32, (N, N), 0)
            col = lax.broadcasted_iota(jnp.int32, (N, N), 1)
            column = jnp.sum(jnp.where(row == col, floor, 0.0), axis=1, keepdims=True)
            depth = lax.broadcasted_iota(jnp.int32, (N, NZ), 1).astype(f32)
            mask = (depth >= column).astype(f32)
            ab = []
            for k, ref in enumerate((sh_ref, sv_ref)):
                shift = scale * ref[here, :] * mask
                shift_ref[k, there, :] = shift
                ab.append(factors(shift))
                ab_ref[2 * k, there, :] = ab[k][0]
                ab_ref[2 * k + 1, there, :] = ab[k][1]
            zeros = jnp.zeros((8, NZ), f32)
            for fr, fi, k in pairs():
                ref, g = (src_ref, 0) if fr < 6 else (adj_ref, 6)
                re, im = times(ab[k], ref[fr - g, here, :], ref[fi - g, here, :])
                for f, value in ((fr, re), (fi, im)):
                    u_ref[f, pl.ds(start, N), :] = value
                    u_ref[f, pl.ds(start + N, 8), :] = zeros
                    v_ref[f, pl.ds(start + N, 8), :] = zeros
            return carry

        lax.fori_loop(0, STEP, plane, 0)

    @pl.when(step > 0)
    def _():
        def plane(j, carry):
            x = (step - 1) * STEP + j
            there = pl.ds(pl.multiple_of(x * N, N), N)
            start = pl.multiple_of(base(x), 8)
            ab = [(ab_ref[2 * k, there, :], ab_ref[2 * k + 1, there, :]) for k in range(2)]
            for fr, fi, k in pairs():
                re, im = times(ab[k], stencil(u_ref, fr, x), stencil(u_ref, fi, x))
                v_ref[fr, pl.ds(start, N), :] = u_ref[fr, pl.ds(start, N), :] + re
                v_ref[fi, pl.ds(start, N), :] = u_ref[fi, pl.ds(start, N), :] + im
            return carry

        lax.fori_loop(0, STEP, plane, 0)

    @pl.when(step == N // STEP)
    def _():
        link_y = [links_ref[0, 2].astype(f32), links_ref[0, 3].astype(f32)]

        def field(f, carry):
            for ref, at in ((u_ref, 0), (v_ref, FACE)):
                out = pl.ds(pl.multiple_of(at + f * N, N), N)
                layer = [ref[f, pl.ds(base(x), N), :] for x in (0, 1, N - 2, N - 1)]
                xl_ref[out, :] = trace(layer[0], layer[1])
                xh_ref[out, :] = trace(layer[3], layer[2])
                for b in range(N // 8):
                    out = pl.ds(pl.multiple_of(at + f * N + b * 8, 8), 8)
                    layer = [ref[f, pl.ds(base(b * 8) + y, 8, stride=PLANE), :] for y in (0, 1, N - 2, N - 1)]
                    yl_ref[out, :] = trace(layer[0], layer[1])
                    yh_ref[out, :] = trace(layer[3], layer[2])
            return carry

        lax.fori_loop(0, NF, field, 0)
        for k in range(2):
            out = slice(X_S + k * N, X_S + (k + 1) * N)
            xl_ref[out, :] = shift_ref[k, 0:N, :]
            xh_ref[out, :] = shift_ref[k, CELLS - N:CELLS, :]
            yl_ref[out, :] = shift_ref[k, pl.ds(0, N, stride=N), :]
            yh_ref[out, :] = shift_ref[k, pl.ds(N - 1, N, stride=N), :]
        for e, y_ref in enumerate((yl_ref, yh_ref)):
            for f in range(NF):
                at = X_R + e * 24 + f * 2
                xl_ref[at:at + 2, :] = y_ref[f * N:f * N + 2, :] * link_y[e]
                xh_ref[at:at + 2, :] = y_ref[f * N + 30:f * N + 32, :] * link_y[e]
            for k in range(2):
                for layer in range(2):
                    at = X_C + e * 4 + k * 2 + layer
                    y = e * (N - 1)
                    low = layer * N + y
                    high = (N - 1 - layer) * N + y
                    xl_ref[at:at + 1, :] = shift_ref[k, low:low + 1, :]
                    xh_ref[at:at + 1, :] = shift_ref[k, high:high + 1, :]
        sub = lax.axis_index("sub")
        odd_x = lax.rem(sub, 2) == 1
        odd_y = lax.rem(lax.div(sub, SX), 2) == 1
        low, high = xl_ref[...], xh_ref[...]
        px0_ref[...] = jnp.where(odd_x, low, high)
        px1_ref[...] = jnp.where(odd_x, high, low)
        low, high = yl_ref[...], yh_ref[...]
        py0_ref[...] = jnp.where(odd_y, low, high)
        py1_ref[...] = jnp.where(odd_y, high, low)


def second_kernel(freq_ref, u_ref, v_ref, ab_ref, w_ref, keep_ref, send_ref):
    step = pl.program_id(0)
    scale = scale_of(freq_ref)
    odd_core = lax.rem(lax.axis_index("freq"), 2) == 1

    def plane(j, carry):
        x = step * STEP + j
        here = pl.ds(pl.multiple_of(j * N, N), N)
        there = pl.ds(pl.multiple_of(x * N, N), N)
        start = pl.multiple_of(base(x), 8)
        ab = [(ab_ref[2 * k, there, :], ab_ref[2 * k + 1, there, :]) for k in range(2)]
        term = [None, None]
        for comp in range(3):
            k = comp // 2
            new = []
            for solve in range(2):
                fr, fi = solve * 6 + comp, solve * 6 + 3 + comp
                re, im = times(ab[k], stencil(v_ref, fr, x), stencil(v_ref, fi, x))
                re = re + u_ref[fr, pl.ds(start, N), :]
                im = im + u_ref[fi, pl.ds(start, N), :]
                w_ref[fr, there, :] = re
                w_ref[fi, there, :] = im
                new.append((re, im))
            product = new[1][0] * new[0][1] + new[1][1] * new[0][0]
            term[k] = product if term[k] is None else term[k] + product
        term_h, term_v = scale * term[0], scale * term[1]
        keep_ref[here, :] = jnp.where(odd_core, term_v, term_h)
        send_ref[here, :] = jnp.where(odd_core, term_h, term_v)
        return carry

    lax.fori_loop(0, STEP, plane, 0)


def edge_kernel(links_ref, ab_ref, rx0_ref, rx1_ref, ty0_ref, ty1_ref, tl_ref, th_ref):
    sub = lax.axis_index("sub")
    odd_x = lax.rem(sub, 2) == 1
    odd_y = lax.rem(lax.div(sub, SX), 2) == 1

    def from_x(side, rows):
        first, second = rx0_ref[rows, :], rx1_ref[rows, :]
        return jnp.where(odd_x, first, second) if side == 0 else jnp.where(odd_x, second, first)

    for e, t_ref in enumerate((tl_ref, th_ref)):
        outer, inner = (0, 1) if e == 0 else (N - 1, N - 2)
        for side in range(2):
            link = links_ref[0, side].astype(f32)
            x = side * (N - 1)
            for fr, fi, k in pairs():
                layers = []
                for y in (outer, inner):
                    at = x * N + y
                    ab = (ab_ref[2 * k, at:at + 1, :], ab_ref[2 * k + 1, at:at + 1, :])
                    re = link * from_x(side, slice(fr * N + y, fr * N + y + 1))
                    im = link * from_x(side, slice(fi * N + y, fi * N + y + 1))
                    layers.append(times(ab, re, im))
                t_ref[side * NF + fr:side * NF + fr + 1, :] = trace(layers[0][0], layers[1][0])
                t_ref[side * NF + fi:side * NF + fi + 1, :] = trace(layers[0][1], layers[1][1])
            at = X_R + e * 24
            t_ref[24 + side * 24:48 + side * 24, :] = from_x(side, slice(at, at + 24))
    low, high = tl_ref[...], th_ref[...]
    ty0_ref[...] = jnp.where(odd_y, low, high)
    ty1_ref[...] = jnp.where(odd_y, high, low)


def boundary_kernel(
    freq_ref, links_ref, u_ref, ab_ref, w_ref, rx0_ref, rx1_ref, ry0_ref, ry1_ref, rt0_ref, rt1_ref,
    planes_ref, rows_ref, keep_ref, send_ref,
):
    scale = scale_of(freq_ref)
    sub = lax.axis_index("sub")
    odd_x = lax.rem(sub, 2) == 1
    odd_y = lax.rem(lax.div(sub, SX), 2) == 1
    odd_core = lax.rem(lax.axis_index("freq"), 2) == 1
    link = [links_ref[0, k].astype(f32) for k in range(4)]
    row = lax.broadcasted_iota(jnp.int32, (N, NZ), 0)

    def pick(odd, side, first_ref, second_ref, rows):
        first, second = first_ref[rows, :], second_ref[rows, :]
        return jnp.where(odd, first, second) if side == 0 else jnp.where(odd, second, first)

    def from_x(side, at, size):
        return pick(odd_x, side, rx0_ref, rx1_ref, slice(at, at + size))

    def from_y(side, at, size):
        return pick(odd_y, side, ry0_ref, ry1_ref, slice(at, at + size))

    def from_t(side, at, size):
        return pick(odd_y, side, rt0_ref, rt1_ref, slice(at, at + size))

    def ends(first, last):
        return jnp.where(row == 0, first, jnp.where(row == N - 1, last, 0.0))

    def ab_plane(k, x):
        return ab_ref[2 * k, x * N:(x + 1) * N, :], ab_ref[2 * k + 1, x * N:(x + 1) * N, :]

    def ab_row(k, y):
        return ab_ref[2 * k, pl.ds(y, N, stride=N), :], ab_ref[2 * k + 1, pl.ds(y, N, stride=N), :]

    near_x = [[factors(from_x(s, X_S + k * N, N)) for k in range(2)] for s in range(2)]
    near_y = [[factors(from_y(s, X_S + k * N, N)) for k in range(2)] for s in range(2)]
    corner = [[[[factors(from_x(s, X_C + e * 4 + k * 2 + layer, 1)) for layer in range(2)]
                for k in range(2)] for e in range(2)] for s in range(2)]

    for fr, fi, k in pairs():
        both = (fr, fi)
        edge, ghost_y = [], []
        for e in range(2):
            outer, inner = (0, 1) if e == 0 else (N - 1, N - 2)
            g1 = [link[2 + e] * from_y(e, f * N, N) for f in both]
            edge.append((g1, times(ab_row(k, outer), *g1)))
            own = [trace(u_ref[f, pl.ds(base(0) + outer, N, stride=PLANE), :],
                         u_ref[f, pl.ds(base(0) + inner, N, stride=PLANE), :]) for f in both]
            back = times(near_y[e][k], *own)
            ghost_y.append([
                link[2 + e] * (from_y(e, FACE + f * N, N) + KEEP * back[c] + ends(from_t(e, f, 1), from_t(e, NF + f, 1)))
                for c, f in enumerate(both)
            ])
        for s in range(2):
            x0, x1, x2 = (0, 1, 2) if s == 0 else (N - 1, N - 2, N - 3)
            g1 = [link[s] * from_x(s, f * N, N) + ends(edge[0][0][c][x0:x0 + 1, :], edge[1][0][c][x0:x0 + 1, :])
                  for c, f in enumerate(both)]
            ab0, ab1 = ab_plane(k, x0), ab_plane(k, x1)
            w0 = times(ab0, *g1)
            own = [trace(u_ref[f, base(x0):base(x0) + N, :], u_ref[f, base(x1):base(x1) + N, :]) for f in both]
            back = times(near_x[s][k], *own)
            corners = []
            for e in range(2):
                layers = []
                for layer in range(2):
                    col = layer if s == 1 else 1 - layer
                    relay = [from_t(e, 24 + s * 24 + f * 2 + col, 1) for f in both]
                    layers.append(times(corner[s][e][k][layer], *relay))
                corners.append([trace(layers[0][c], layers[1][c]) for c in range(2)])
            rhs0, rhs1 = [], []
            for c, f in enumerate(both):
                ghost = link[s] * (from_x(s, FACE + f * N, N) + KEEP * back[c] + ends(corners[0][c], corners[1][c]))
                m1 = ends(edge[0][1][c][x1:x1 + 1, :], edge[1][1][c][x1:x1 + 1, :])
                m2 = ends(edge[0][1][c][x2:x2 + 1, :], edge[1][1][c][x2:x2 + 1, :])
                side0 = ends(ghost_y[0][c][x0:x0 + 1, :], ghost_y[1][c][x0:x0 + 1, :])
                side1 = ends(ghost_y[0][c][x1:x1 + 1, :], ghost_y[1][c][x1:x1 + 1, :])
                rhs0.append(row_neighbours(w0[c]) + lane_neighbours(w0[c]) + m1 + ghost + side0)
                rhs1.append(w0[c] + m2 + row_neighbours(m1) + lane_neighbours(m1) + side1)
            fix0, fix1 = times(ab0, *rhs0), times(ab1, *rhs1)
            at0, at1 = (0, 1) if s == 0 else (3, 2)
            for c, f in enumerate(both):
                planes_ref[f, at0 * N:(at0 + 1) * N, :] = w_ref[f, x0 * N:(x0 + 1) * N, :] + fix0[c]
                planes_ref[f, at1 * N:(at1 + 1) * N, :] = w_ref[f, x1 * N:(x1 + 1) * N, :] + fix1[c]
        for e in range(2):
            outer, inner = (0, 1) if e == 0 else (N - 1, N - 2)
            w0 = edge[e][1]
            rhs = [row_neighbours(w0[c]) + lane_neighbours(w0[c]) + ghost_y[e][c] for c in range(2)]
            fix0 = times(ab_row(k, outer), *rhs)
            fix1 = times(ab_row(k, inner), *w0)
            at0, at1 = (0, 1) if e == 0 else (3, 2)
            for c, f in enumerate(both):
                rows_ref[f, at0 * N:(at0 + 1) * N, :] = w_ref[f, pl.ds(outer, N, stride=N), :] + fix0[c]
                rows_ref[f, at1 * N:(at1 + 1) * N, :] = w_ref[f, pl.ds(inner, N, stride=N), :] + fix1[c]
    for ref, at in ((planes_ref, 0), (rows_ref, 4 * N)):
        term = [None, None]
        for comp in range(3):
            product = ref[6 + comp] * ref[3 + comp] + ref[9 + comp] * ref[comp]
            term[comp // 2] = product if comp % 2 == 0 else term[0] + product
        term_h, term_v = scale * term[0], scale * term[1]
        keep_ref[at:at + 4 * N, :] = jnp.where(odd_core, term_v, term_h)
        send_ref[at:at + 4 * N, :] = jnp.where(odd_core, term_h, term_v)


def put_boundary(step, block_ref, index, planes, rows):
    for at, y in enumerate((0, 1, N - 2, N - 1)):
        block_ref[(*index, pl.ds(y, STEP, stride=N), slice(None))] = rows(at)

    @pl.when(step == 0)
    def _():
        block_ref[(*index, slice(0, 2 * N), slice(None))] = planes(0)

    @pl.when(step == N // STEP - 1)
    def _():
        block_ref[(*index, slice(BLOCK - 2 * N, BLOCK), slice(None))] = planes(2 * N)


def field_kernel(w_ref, planes_ref, rows_ref, out_ref):
    step = pl.program_id(0)
    out_ref[...] = w_ref[0:6, pl.ds(pl.multiple_of(step * BLOCK, BLOCK), BLOCK), :]
    for f in range(6):
        put_boundary(
            step, out_ref, (f,),
            lambda at, f=f: planes_ref[f, at:at + 2 * N, :],
            lambda at, f=f: rows_ref[f, pl.ds(pl.multiple_of(at * N + step * STEP, 8), STEP), :],
        )


def gradient_kernel(mine_ref, other_ref, mine_b_ref, other_b_ref, ab_ref, sh_ref, sv_ref, gh_ref, gv_ref, total_ref):
    step = pl.program_id(0)
    odd_core = lax.rem(lax.axis_index("freq"), 2) == 1
    mask = (ab_ref[0, pl.ds(pl.multiple_of(step * BLOCK, BLOCK), BLOCK), :] > 0.0).astype(f32)
    for k, (sigma_ref, out_ref) in enumerate(((sh_ref, gh_ref), (sv_ref, gv_ref))):
        first = odd_core if k == 1 else jnp.logical_not(odd_core)
        total_ref[...] = jnp.where(first, mine_ref[...], other_ref[...])

        def boundary(rows):
            return jnp.where(first, mine_b_ref[rows, :], other_b_ref[rows, :])

        put_boundary(
            step, total_ref, (),
            lambda at: boundary(slice(at, at + 2 * N)),
            lambda at: boundary(pl.ds(pl.multiple_of((4 + at) * N + step * STEP, 8), STEP)),
        )
        out_ref[...] = sigma_ref[...] * mask * total_ref[...]


def swap_pairs(axis, odd):
    pairs_of = []
    for i in range(SUBS):
        at = [i % SX, i // SX]
        at[axis] += 1 if at[axis] % 2 == odd else -1
        if 0 <= at[axis] < SX:
            pairs_of.append((i, at[1] * SX + at[0]))
    return pairs_of


def swap(value, axis, odd):
    return lax.ppermute(value, "sub", swap_pairs(axis, odd))


def swap_freq(value, flip):
    return lax.ppermute(value, "freq", [(i, i ^ flip) for i in range(4)])


def sds(*shape):
    return jax.ShapeDtypeStruct(shape, f32)


def on_device(source, adjoint_source, sigma_h, sigma_v, seafloor, links, freq_index):
    steps = N // STEP
    src = source.reshape(6, CELLS, NZ)
    adj = adjoint_source.reshape(6, CELLS, NZ)
    cond_h = sigma_h.reshape(CELLS, NZ)
    cond_v = sigma_v.reshape(CELLS, NZ)
    floor = seafloor.reshape(N, N)

    def block3(size):
        return pl.BlockSpec((size, BLOCK, NZ), lambda i: (0, jnp.minimum(i, steps - 1), 0))

    block2 = pl.BlockSpec((BLOCK, NZ), lambda i: (jnp.minimum(i, steps - 1), 0))
    u, v, ab, px0, px1, py0, py1 = pl.pallas_call(
        first_kernel,
        grid=(steps + 1,),
        in_specs=[whole(pltpu.SMEM), whole(pltpu.SMEM), whole(), block3(6), block3(6), block2, block2],
        out_specs=[whole()] * 7,
        out_shape=[
            pltpu.VMEM((NF, ROWS, NZ), f32), pltpu.VMEM((NF, ROWS, NZ), f32), pltpu.VMEM((4, CELLS, NZ), f32),
            sds(X_ROWS, NZ), sds(X_ROWS, NZ), sds(Y_ROWS, NZ), sds(Y_ROWS, NZ),
        ],
        scratch_shapes=[pltpu.VMEM((2, CELLS, NZ), f32)]
        + [pltpu.VMEM((X_ROWS, NZ), f32)] * 2 + [pltpu.VMEM((Y_ROWS, NZ), f32)] * 2,
        compiler_params=params(1),
        cost_estimate=cost(30 * NF * CELLS * NZ, 7 * 2**20),
        name="first",
    )(freq_index, links, floor, src, adj, cond_h, cond_v)

    ry1 = swap(py1, 1, 1)
    ry0 = swap(py0, 1, 0)
    rx0 = swap(px0, 0, 0)
    rx1 = swap(px1, 0, 1)

    w, keep, send = pl.pallas_call(
        second_kernel,
        grid=(steps,),
        in_specs=[whole(pltpu.SMEM), whole(), whole(), whole()],
        out_specs=[whole(), block2, block2],
        out_shape=[pltpu.VMEM((NF, CELLS, NZ), f32), sds(CELLS, NZ), sds(CELLS, NZ)],
        compiler_params=params(1),
        cost_estimate=cost(20 * NF * CELLS * NZ, 20 * 2**20),
        name="second",
    )(freq_index, u, v, ab)

    ty0, ty1 = pl.pallas_call(
        edge_kernel,
        in_specs=[whole(pltpu.SMEM)] + [whole()] * 3,
        out_specs=[whole()] * 2,
        out_shape=[sds(T_ROWS, NZ)] * 2,
        scratch_shapes=[pltpu.VMEM((T_ROWS, NZ), f32)] * 2,
        compiler_params=params(),
        cost_estimate=cost(10**5, 2**20),
        name="edges",
    )(links, ab, rx0, rx1)
    rt1 = swap(ty1, 1, 1)
    rt0 = swap(ty0, 1, 0)

    mine = keep + swap_freq(send, 1)
    mine = mine + swap_freq(mine, 2)
    other = swap_freq(mine, 1)

    planes, rows, keep_b, send_b = pl.pallas_call(
        boundary_kernel,
        in_specs=[whole(pltpu.SMEM)] * 2 + [whole()] * 9,
        out_specs=[whole()] * 4,
        out_shape=[pltpu.VMEM((NF, 4 * N, NZ), f32)] * 2 + [sds(8 * N, NZ)] * 2,
        compiler_params=params(),
        cost_estimate=cost(10**7, 4 * 2**20),
        name="boundary",
    )(freq_index, links, u, ab, w, rx0, rx1, ry0, ry1, rt0, rt1)

    mine_b = keep_b + swap_freq(send_b, 1)
    mine_b = mine_b + swap_freq(mine_b, 2)
    other_b = swap_freq(mine_b, 1)

    forward = pl.pallas_call(
        field_kernel,
        grid=(steps,),
        in_specs=[whole()] * 3,
        out_specs=block3(6),
        out_shape=sds(6, CELLS, NZ),
        compiler_params=params(1),
        cost_estimate=cost(10**6, 6 * 2**20),
        name="field",
    )(w, planes, rows)

    grad_h, grad_v = pl.pallas_call(
        gradient_kernel,
        grid=(steps,),
        in_specs=[block2, block2, whole(), whole(), whole(), block2, block2],
        out_specs=[block2, block2],
        out_shape=[sds(CELLS, NZ)] * 2,
        scratch_shapes=[pltpu.VMEM((BLOCK, NZ), f32)],
        compiler_params=params(1),
        cost_estimate=cost(10**6, 4 * 2**20),
        name="gradient",
    )(mine, other, mine_b, other_b, ab, cond_h, cond_v)

    return (
        forward.reshape(1, 1, 2, 3, N, N, NZ),
        grad_h.reshape(1, N, N, NZ),
        grad_v.reshape(1, N, N, NZ),
    )


def solution(mesh):
    return jax.shard_map(
        on_device,
        mesh=mesh,
        in_specs=(
            P("sub", None, None, None, None, None),
            P("freq", "sub", None, None, None, None, None),
            P("sub", None, None, None),
            P("sub", None, None, None),
            P("sub", None, None),
            P("sub", None),
            P("freq"),
        ),
        out_specs=(
            P("freq", "sub", None, None, None, None, None),
            P("sub", None, None, None),
            P("sub", None, None, None),
        ),
        check_vma=False,
    )
```

```python
import jax
import jax.numpy as jnp
from jax import lax
from jax.experimental import pallas as pl
from jax.experimental.pallas import tpu as pltpu
from jax.sharding import PartitionSpec as P

SX = 8
SUBS = 64
N = 32
NZ = 128
PLANE = 40
ROWS = 34 * PLANE
STEP = 8
BLOCK = STEP * N
CELLS = N * N
NF = 12
FACE = NF * N
X_S, X_R, X_C, X_ROWS = 2 * FACE, 2 * FACE + 64, 2 * FACE + 112, 2 * FACE + 120
Y_ROWS = 2 * FACE + 64
T_ROWS = 72

P_ROBIN = 0.25
OMEGA0 = 0.5
KEEP = 1.0 + P_ROBIN
f32 = jnp.float32


def whole(space=pltpu.VMEM):
    return pl.BlockSpec(memory_space=space)


def params(mib):
    return pltpu.CompilerParams(vmem_limit_bytes=mib * 2**20)


def in_hbm(value):
    return pltpu.with_memory_space_constraint(value, pltpu.HBM)


def cost(flops, size):
    return pl.CostEstimate(flops=flops, bytes_accessed=size, transcendentals=0)


def base(x):
    return (x + 1) * PLANE


def scale_of(freq_ref):
    return OMEGA0 * jnp.left_shift(jnp.int32(1), freq_ref[0]).astype(f32)


def link_of(links_ref, k):
    return links_ref[0:1, k:k + 1].astype(f32)


def lane_neighbours(u):
    lane = lax.broadcasted_iota(jnp.int32, u.shape, 1)
    before = jnp.where(lane == 0, 0.0, pltpu.roll(u, 1, 1))
    after = jnp.where(lane == NZ - 1, 0.0, pltpu.roll(u, NZ - 1, 1))
    return before + after


def row_neighbours(u):
    row = lax.broadcasted_iota(jnp.int32, u.shape, 0)
    before = jnp.where(row == 0, 0.0, pltpu.roll(u, 1, 0))
    after = jnp.where(row == N - 1, 0.0, pltpu.roll(u, N - 1, 0))
    return before + after


def factors(shift):
    inverse = 1.0 / (36.0 + shift * shift)
    return jnp.where(shift > 0.0, 6.0 * inverse, 0.0), shift * inverse


def times(ab, re, im):
    a, b = ab
    return a * re + b * im, a * im - b * re


def pairs():
    for solve in range(2):
        for comp in range(3):
            yield solve * 6 + comp, solve * 6 + 3 + comp, comp // 2


def trace(outer, inner):
    return KEEP * outer - P_ROBIN * inner


def stencil(ref, f, x):
    start = base(x)
    centre = ref[f, pl.ds(start, N), :]
    total = ref[f, pl.ds(start - PLANE, N), :] + ref[f, pl.ds(start + PLANE, N), :]
    total = total + (ref[f, pl.ds(start - 1, N), :] + ref[f, pl.ds(start + 1, N), :])
    return total + lane_neighbours(centre)


def floor_column(floor_ref, x, first, size):
    floor = floor_ref[pl.ds(x, 1), :].astype(f32)
    row = lax.broadcasted_iota(jnp.int32, (size, N), 0) + first
    col = lax.broadcasted_iota(jnp.int32, (size, N), 1)
    return jnp.sum(jnp.where(row == col, floor, 0.0), axis=1, keepdims=True)


def mask_of(column):
    depth = lax.broadcasted_iota(jnp.int32, (column.shape[0], NZ), 1).astype(f32)
    return (depth >= column).astype(f32)


def parity():
    sub = lax.axis_index("sub")
    return lax.rem(sub, 2) == 1, lax.rem(lax.div(sub, SX), 2) == 1


def face(out_ref, shift, field, keep=None):
    ab = [[factors(value) for value in layer] for layer in shift]
    for k in range(2):
        out_ref[X_S + k * N:X_S + (k + 1) * N, :] = shift[0][k]
    for fr, fi, k in pairs():
        u = [times(ab[l][k], field(fr, l), field(fi, l)) for l in range(3)]
        v = []
        for l in range(2):
            near = [u[l + 1][c] if l == 0 else u[0][c] + u[2][c] for c in range(2)]
            total = [near[c] + row_neighbours(u[l][c]) + lane_neighbours(u[l][c]) for c in range(2)]
            new = times(ab[l][k], *total)
            v.append([u[l][c] + new[c] for c in range(2)])
        for c, f in enumerate((fr, fi)):
            out_ref[f * N:(f + 1) * N, :] = trace(u[0][c], u[1][c])
            out_ref[FACE + f * N:FACE + (f + 1) * N, :] = trace(v[0][c], v[1][c])
            if keep is not None:
                keep(f, u[0][c], u[1][c])


def strip_kernel(
    freq_ref, links_ref, floor_ref,
    srcx_ref, adjx_ref, shx_ref, svx_ref, srcy_ref, adjy_ref, shy_ref, svy_ref,
    px0_ref, px1_ref, py0_ref, py1_ref, xl_ref, xh_ref, yl_ref, yh_ref,
):
    step = pl.program_id(0)
    scale = scale_of(freq_ref)
    odd_x, odd_y = parity()
    fields = [ref.reshape(6, N * 8, NZ) for ref in (srcy_ref, adjy_ref)]
    sigmas = [ref.reshape(N * 8, NZ) for ref in (shy_ref, svy_ref)]

    def side(s, x_ref, y_ref):
        def plane(l):
            return slice((3 - l) * N, (4 - l) * N) if s else slice(l * N, (l + 1) * N)

        def line(l):
            return pl.ds(7 - l if s else l, N, stride=8)

        def field_x(f, l):
            return srcx_ref[f, plane(l), :] if f < 6 else adjx_ref[f - 6, plane(l), :]

        def field_y(f, l):
            return fields[f // 6][f % 6, line(l), :]

        def relay(f, outer, inner):
            for e in range(2):
                for l, value in enumerate((outer, inner)):
                    at = X_R + e * 24 + f * 2 + l
                    row = [value[y:y + 1, :] for y in ((N - 1, N - 2) if e else (0, 1))]
                    x_ref[at:at + 1, :] = link_of(links_ref, 2 + e) * trace(*row)

        layers = [N - 1 - l if s else l for l in range(3)]
        masks = [mask_of(floor_column(floor_ref, x, 0, N)) for x in layers]
        shift = [[scale * ref[plane(l), :] * masks[l] for ref in (shx_ref, svx_ref)] for l in range(3)]
        face(x_ref, shift, field_x, relay)
        for end in range(2):
            for k in range(2):
                for l in range(2):
                    at = X_C + end * 4 + k * 2 + l
                    x_ref[at:at + 1, :] = shift[l][k][end * (N - 1):end * (N - 1) + 1, :]
        masks = [mask_of(floor_ref[:, y:y + 1].astype(f32)) for y in layers]
        shift = [[scale * ref[line(l), :] * masks[l] for ref in sigmas] for l in range(3)]
        face(y_ref, shift, field_y)

    @pl.when(step == 0)
    def _():
        side(0, xl_ref, yl_ref)

    @pl.when(step == 1)
    def _():
        side(1, xh_ref, yh_ref)
        low, high = xl_ref[...], xh_ref[...]
        px0_ref[...] = jnp.where(odd_x, low, high)
        px1_ref[...] = jnp.where(odd_x, high, low)
        low, high = yl_ref[...], yh_ref[...]
        py0_ref[...] = jnp.where(odd_y, low, high)
        py1_ref[...] = jnp.where(odd_y, high, low)


def edge_kernel(links_ref, ab_ref, rx0_ref, rx1_ref, ty0_ref, ty1_ref, tl_ref, th_ref):
    odd_x, odd_y = parity()

    def from_x(side, rows):
        first, second = rx0_ref[rows, :], rx1_ref[rows, :]
        return jnp.where(odd_x, first, second) if side == 0 else jnp.where(odd_x, second, first)

    for e, t_ref in enumerate((tl_ref, th_ref)):
        outer, inner = (0, 1) if e == 0 else (N - 1, N - 2)
        for side in range(2):
            link = link_of(links_ref, side)
            x = side * (N - 1)
            for fr, fi, k in pairs():
                layers = []
                for y in (outer, inner):
                    at = x * N + y
                    ab = (ab_ref[2 * k, at:at + 1, :], ab_ref[2 * k + 1, at:at + 1, :])
                    re = link * from_x(side, slice(fr * N + y, fr * N + y + 1))
                    im = link * from_x(side, slice(fi * N + y, fi * N + y + 1))
                    layers.append(times(ab, re, im))
                t_ref[side * NF + fr:side * NF + fr + 1, :] = trace(layers[0][0], layers[1][0])
                t_ref[side * NF + fi:side * NF + fi + 1, :] = trace(layers[0][1], layers[1][1])
            at = X_R + e * 24
            t_ref[24 + side * 24:48 + side * 24, :] = from_x(side, slice(at, at + 24))
    low, high = tl_ref[...], th_ref[...]
    ty0_ref[...] = jnp.where(odd_y, low, high)
    ty1_ref[...] = jnp.where(odd_y, high, low)


def solve_kernel(
    freq_ref, floor_ref, src_ref, adj_ref, sh_ref, sv_ref,
    u_ref, ab_ref, w_ref, keep_ref, send_ref, v_ref,
):
    step = pl.program_id(0)
    scale = scale_of(freq_ref)
    odd_core = lax.rem(lax.axis_index("freq"), 2) == 1

    @pl.when(step == 0)
    def _():
        zeros = jnp.zeros((PLANE, NZ), f32)
        for f in range(NF):
            for ref in (u_ref, v_ref):
                ref[f, 0:PLANE, :] = zeros
                ref[f, ROWS - PLANE:ROWS, :] = zeros

    @pl.when(step < N // STEP)
    def _():
        def plane(j, carry):
            x = step * STEP + j
            here = pl.ds(pl.multiple_of(j * N, N), N)
            there = pl.ds(pl.multiple_of(x * N, N), N)
            start = pl.multiple_of(base(x), 8)
            mask = mask_of(floor_column(floor_ref, x, 0, N))
            ab = []
            for k, ref in enumerate((sh_ref, sv_ref)):
                ab.append(factors(scale * ref[here, :] * mask))
                ab_ref[2 * k, there, :] = ab[k][0]
                ab_ref[2 * k + 1, there, :] = ab[k][1]
            zeros = jnp.zeros((8, NZ), f32)
            for fr, fi, k in pairs():
                ref, g = (src_ref, 0) if fr < 6 else (adj_ref, 6)
                re, im = times(ab[k], ref[fr - g, here, :], ref[fi - g, here, :])
                for f, value in ((fr, re), (fi, im)):
                    u_ref[f, pl.ds(start, N), :] = value
                    u_ref[f, pl.ds(start + N, 8), :] = zeros
                    v_ref[f, pl.ds(start + N, 8), :] = zeros
            return carry

        lax.fori_loop(0, STEP, plane, 0, unroll=4)

    @pl.when(step > 0)
    def _():
        def plane(j, carry):
            x = (step - 1) * STEP + j
            there = pl.ds(pl.multiple_of(x * N, N), N)
            start = pl.multiple_of(base(x), 8)
            ab = [(ab_ref[2 * k, there, :], ab_ref[2 * k + 1, there, :]) for k in range(2)]
            for fr, fi, k in pairs():
                re, im = times(ab[k], stencil(u_ref, fr, x), stencil(u_ref, fi, x))
                v_ref[fr, pl.ds(start, N), :] = u_ref[fr, pl.ds(start, N), :] + re
                v_ref[fi, pl.ds(start, N), :] = u_ref[fi, pl.ds(start, N), :] + im
            return carry

        lax.fori_loop(0, STEP, plane, 0, unroll=4)

    @pl.when(step == N // STEP)
    def _():
        def plane(x, carry):
            there = pl.ds(pl.multiple_of(x * N, N), N)
            start = pl.multiple_of(base(x), 8)
            ab = [(ab_ref[2 * k, there, :], ab_ref[2 * k + 1, there, :]) for k in range(2)]
            term = [None, None]
            for comp in range(3):
                k = comp // 2
                new = []
                for solve in range(2):
                    fr, fi = solve * 6 + comp, solve * 6 + 3 + comp
                    re, im = times(ab[k], stencil(v_ref, fr, x), stencil(v_ref, fi, x))
                    re = re + u_ref[fr, pl.ds(start, N), :]
                    im = im + u_ref[fi, pl.ds(start, N), :]
                    w_ref[fr, there, :] = re
                    w_ref[fi, there, :] = im
                    new.append((re, im))
                product = new[1][0] * new[0][1] + new[1][1] * new[0][0]
                term[k] = product if term[k] is None else term[k] + product
            term_h, term_v = scale * term[0], scale * term[1]
            keep_ref[there, :] = jnp.where(odd_core, term_v, term_h)
            send_ref[there, :] = jnp.where(odd_core, term_h, term_v)
            return carry

        lax.fori_loop(0, N, plane, 0, unroll=4)


def boundary_kernel(
    freq_ref, links_ref, u_ref, ab_ref, w_ref, rx0_ref, rx1_ref, ry0_ref, ry1_ref, rt0_ref, rt1_ref,
    planes_ref, rows_ref, keep_ref, send_ref,
):
    scale = scale_of(freq_ref)
    odd_x, odd_y = parity()
    odd_core = lax.rem(lax.axis_index("freq"), 2) == 1
    link = [link_of(links_ref, k) for k in range(4)]
    row = lax.broadcasted_iota(jnp.int32, (N, NZ), 0)

    def pick(odd, side, first_ref, second_ref, rows):
        first, second = first_ref[rows, :], second_ref[rows, :]
        return jnp.where(odd, first, second) if side == 0 else jnp.where(odd, second, first)

    def from_x(side, at, size):
        return pick(odd_x, side, rx0_ref, rx1_ref, slice(at, at + size))

    def from_y(side, at, size):
        return pick(odd_y, side, ry0_ref, ry1_ref, slice(at, at + size))

    def from_t(side, at, size):
        return pick(odd_y, side, rt0_ref, rt1_ref, slice(at, at + size))

    def ends(first, last):
        return jnp.where(row == 0, first, jnp.where(row == N - 1, last, 0.0))

    def ab_plane(k, x):
        return ab_ref[2 * k, x * N:(x + 1) * N, :], ab_ref[2 * k + 1, x * N:(x + 1) * N, :]

    def ab_row(k, y):
        return ab_ref[2 * k, pl.ds(y, N, stride=N), :], ab_ref[2 * k + 1, pl.ds(y, N, stride=N), :]

    near_x = [[factors(from_x(s, X_S + k * N, N)) for k in range(2)] for s in range(2)]
    near_y = [[factors(from_y(s, X_S + k * N, N)) for k in range(2)] for s in range(2)]
    corner = [[[[factors(from_x(s, X_C + e * 4 + k * 2 + layer, 1)) for layer in range(2)]
                for k in range(2)] for e in range(2)] for s in range(2)]

    for fr, fi, k in pairs():
        both = (fr, fi)
        edge, ghost_y = [], []
        for e in range(2):
            outer, inner = (0, 1) if e == 0 else (N - 1, N - 2)
            g1 = [link[2 + e] * from_y(e, f * N, N) for f in both]
            edge.append((g1, times(ab_row(k, outer), *g1)))
            own = [trace(u_ref[f, pl.ds(base(0) + outer, N, stride=PLANE), :],
                         u_ref[f, pl.ds(base(0) + inner, N, stride=PLANE), :]) for f in both]
            back = times(near_y[e][k], *own)
            ghost_y.append([
                link[2 + e] * (from_y(e, FACE + f * N, N) + KEEP * back[c] + ends(from_t(e, f, 1), from_t(e, NF + f, 1)))
                for c, f in enumerate(both)
            ])
        for s in range(2):
            x0, x1, x2 = (0, 1, 2) if s == 0 else (N - 1, N - 2, N - 3)
            g1 = [link[s] * from_x(s, f * N, N) + ends(edge[0][0][c][x0:x0 + 1, :], edge[1][0][c][x0:x0 + 1, :])
                  for c, f in enumerate(both)]
            ab0, ab1 = ab_plane(k, x0), ab_plane(k, x1)
            w0 = times(ab0, *g1)
            own = [trace(u_ref[f, base(x0):base(x0) + N, :], u_ref[f, base(x1):base(x1) + N, :]) for f in both]
            back = times(near_x[s][k], *own)
            corners = []
            for e in range(2):
                layers = []
                for layer in range(2):
                    relay = [from_t(e, 24 + s * 24 + f * 2 + layer, 1) for f in both]
                    layers.append(times(corner[s][e][k][layer], *relay))
                corners.append([trace(layers[0][c], layers[1][c]) for c in range(2)])
            rhs0, rhs1 = [], []
            for c, f in enumerate(both):
                ghost = link[s] * (from_x(s, FACE + f * N, N) + KEEP * back[c] + ends(corners[0][c], corners[1][c]))
                m1 = ends(edge[0][1][c][x1:x1 + 1, :], edge[1][1][c][x1:x1 + 1, :])
                m2 = ends(edge[0][1][c][x2:x2 + 1, :], edge[1][1][c][x2:x2 + 1, :])
                side0 = ends(ghost_y[0][c][x0:x0 + 1, :], ghost_y[1][c][x0:x0 + 1, :])
                side1 = ends(ghost_y[0][c][x1:x1 + 1, :], ghost_y[1][c][x1:x1 + 1, :])
                rhs0.append(row_neighbours(w0[c]) + lane_neighbours(w0[c]) + m1 + ghost + side0)
                rhs1.append(w0[c] + m2 + row_neighbours(m1) + lane_neighbours(m1) + side1)
            fix0, fix1 = times(ab0, *rhs0), times(ab1, *rhs1)
            at0, at1 = (0, 1) if s == 0 else (3, 2)
            for c, f in enumerate(both):
                planes_ref[f, at0 * N:(at0 + 1) * N, :] = w_ref[f, x0 * N:(x0 + 1) * N, :] + fix0[c]
                planes_ref[f, at1 * N:(at1 + 1) * N, :] = w_ref[f, x1 * N:(x1 + 1) * N, :] + fix1[c]
        for e in range(2):
            outer, inner = (0, 1) if e == 0 else (N - 1, N - 2)
            w0 = edge[e][1]
            rhs = [row_neighbours(w0[c]) + lane_neighbours(w0[c]) + ghost_y[e][c] for c in range(2)]
            fix0 = times(ab_row(k, outer), *rhs)
            fix1 = times(ab_row(k, inner), *w0)
            at0, at1 = (0, 1) if e == 0 else (3, 2)
            for c, f in enumerate(both):
                rows_ref[f, at0 * N:(at0 + 1) * N, :] = w_ref[f, pl.ds(outer, N, stride=N), :] + fix0[c]
                rows_ref[f, at1 * N:(at1 + 1) * N, :] = w_ref[f, pl.ds(inner, N, stride=N), :] + fix1[c]
    for ref, at in ((planes_ref, 0), (rows_ref, 4 * N)):
        term = [None, None]
        for comp in range(3):
            product = ref[6 + comp] * ref[3 + comp] + ref[9 + comp] * ref[comp]
            term[comp // 2] = product if comp % 2 == 0 else term[0] + product
        term_h, term_v = scale * term[0], scale * term[1]
        keep_ref[at:at + 4 * N, :] = jnp.where(odd_core, term_v, term_h)
        send_ref[at:at + 4 * N, :] = jnp.where(odd_core, term_h, term_v)


def put_boundary(step, block_ref, index, planes, rows):
    for at, y in enumerate((0, 1, N - 2, N - 1)):
        block_ref[(*index, pl.ds(y, STEP, stride=N), slice(None))] = rows(at)

    @pl.when(step == 0)
    def _():
        block_ref[(*index, slice(0, 2 * N), slice(None))] = planes(0)

    @pl.when(step == N // STEP - 1)
    def _():
        block_ref[(*index, slice(BLOCK - 2 * N, BLOCK), slice(None))] = planes(2 * N)


def field_kernel(w_ref, planes_ref, rows_ref, out_ref):
    step = pl.program_id(0)
    out_ref[...] = w_ref[0:6, pl.ds(pl.multiple_of(step * BLOCK, BLOCK), BLOCK), :]
    for f in range(6):
        put_boundary(
            step, out_ref, (f,),
            lambda at, f=f: planes_ref[f, at:at + 2 * N, :],
            lambda at, f=f: rows_ref[f, pl.ds(pl.multiple_of(at * N + step * STEP, 8), STEP), :],
        )


def gradient_kernel(mine_ref, other_ref, mine_b_ref, other_b_ref, ab_ref, sh_ref, sv_ref, gh_ref, gv_ref, total_ref):
    step = pl.program_id(0)
    odd_core = lax.rem(lax.axis_index("freq"), 2) == 1
    mask = (ab_ref[0, pl.ds(pl.multiple_of(step * BLOCK, BLOCK), BLOCK), :] > 0.0).astype(f32)
    for k, (sigma_ref, out_ref) in enumerate(((sh_ref, gh_ref), (sv_ref, gv_ref))):
        first = odd_core if k == 1 else jnp.logical_not(odd_core)
        total_ref[...] = jnp.where(first, mine_ref[...], other_ref[...])

        def boundary(rows):
            return jnp.where(first, mine_b_ref[rows, :], other_b_ref[rows, :])

        put_boundary(
            step, total_ref, (),
            lambda at: boundary(slice(at, at + 2 * N)),
            lambda at: boundary(pl.ds(pl.multiple_of((4 + at) * N + step * STEP, 8), STEP)),
        )
        out_ref[...] = sigma_ref[...] * mask * total_ref[...]


def swap_pairs(axis, odd):
    pairs_of = []
    for i in range(SUBS):
        at = [i % SX, i // SX]
        at[axis] += 1 if at[axis] % 2 == odd else -1
        if 0 <= at[axis] < SX:
            pairs_of.append((i, at[1] * SX + at[0]))
    return pairs_of


def swap(value, axis, odd):
    return lax.ppermute(value, "sub", swap_pairs(axis, odd))


def swap_freq(value, flip):
    return lax.ppermute(value, "freq", [(i, i ^ flip) for i in range(4)])


def sds(*shape):
    return jax.ShapeDtypeStruct(shape, f32)


def on_device(source, adjoint_source, sigma_h, sigma_v, seafloor, links, freq_index):
    steps = N // STEP
    src = in_hbm(source.reshape(6, N, N, NZ))
    adj = in_hbm(adjoint_source.reshape(6, N, N, NZ))
    cond_h = sigma_h.reshape(CELLS, NZ)
    cond_v = sigma_v.reshape(CELLS, NZ)
    cond_h4 = in_hbm(sigma_h.reshape(N, N, NZ))
    cond_v4 = in_hbm(sigma_v.reshape(N, N, NZ))
    floor = in_hbm(seafloor.reshape(N, N))
    links = in_hbm(links)
    smem = whole(pltpu.SMEM)

    def block3(size):
        return pl.BlockSpec((size, BLOCK, NZ), lambda i: (0, jnp.minimum(i, steps - 1), 0))

    block2 = pl.BlockSpec((BLOCK, NZ), lambda i: (jnp.minimum(i, steps - 1), 0))

    flat_src, flat_adj = in_hbm(source.reshape(6, CELLS, NZ)), in_hbm(adjoint_source.reshape(6, CELLS, NZ))
    flat_h, flat_v = in_hbm(cond_h), in_hbm(cond_v)
    last = N // 4 - 1
    field_x = pl.BlockSpec((6, 4 * N, NZ), lambda i: (0, i * last, 0))
    sigma_x = pl.BlockSpec((4 * N, NZ), lambda i: (i * last, 0))
    field_y = pl.BlockSpec((6, N, 8, NZ), lambda i: (0, 0, i * (N // 8 - 1), 0))
    sigma_y = pl.BlockSpec((N, 8, NZ), lambda i: (0, i * (N // 8 - 1), 0))
    px0, px1, py0, py1 = pl.pallas_call(
        strip_kernel,
        grid=(2,),
        in_specs=[smem] + [whole()] * 2 + [field_x, field_x, sigma_x, sigma_x, field_y, field_y, sigma_y, sigma_y],
        out_specs=[whole()] * 4,
        out_shape=[sds(X_ROWS, NZ), sds(X_ROWS, NZ), sds(Y_ROWS, NZ), sds(Y_ROWS, NZ)],
        scratch_shapes=[pltpu.VMEM((X_ROWS, NZ), f32)] * 2 + [pltpu.VMEM((Y_ROWS, NZ), f32)] * 2,
        compiler_params=params(14),
        cost_estimate=cost(10**6, 12 * 2**20),
        name="strips",
    )(freq_index, links, floor, flat_src, flat_adj, flat_h, flat_v, src, adj, cond_h4, cond_v4)
    ry1 = swap(py1, 1, 1)
    ry0 = swap(py0, 1, 0)
    rx1 = swap(px1, 0, 1)
    rx0 = swap(px0, 0, 0)

    u, ab, w, keep, send = pl.pallas_call(
        solve_kernel,
        grid=(steps + 1,),
        in_specs=[smem, whole(), block3(6), block3(6), block2, block2],
        out_specs=[whole()] * 5,
        out_shape=[
            pltpu.VMEM((NF, ROWS, NZ), f32), pltpu.VMEM((4, CELLS, NZ), f32), pltpu.VMEM((NF, CELLS, NZ), f32),
            sds(CELLS, NZ), sds(CELLS, NZ),
        ],
        scratch_shapes=[pltpu.VMEM((NF, ROWS, NZ), f32)],
        compiler_params=params(16),
        cost_estimate=cost(60 * NF * CELLS * NZ, 40 * 2**20),
        name="solve",
    )(freq_index, floor, flat_src, flat_adj, flat_h, flat_v)

    ty0, ty1 = pl.pallas_call(
        edge_kernel,
        in_specs=[whole()] * 4,
        out_specs=[whole()] * 2,
        out_shape=[sds(T_ROWS, NZ)] * 2,
        scratch_shapes=[pltpu.VMEM((T_ROWS, NZ), f32)] * 2,
        compiler_params=params(4),
        cost_estimate=cost(10**5, 10**6),
        name="edges",
    )(links, ab, rx0, rx1)
    rt1 = swap(ty1, 1, 1)
    rt0 = swap(ty0, 1, 0)

    send, ry0, ry1, rt0, rt1 = lax.optimization_barrier((send, ry0, ry1, rt0, rt1))
    mine = keep + swap_freq(send, 1)
    partner = swap_freq(mine, 2)

    planes, rows, keep_b, send_b = pl.pallas_call(
        boundary_kernel,
        in_specs=[smem] + [whole()] * 10,
        out_specs=[whole()] * 4,
        out_shape=[pltpu.VMEM((NF, 4 * N, NZ), f32)] * 2 + [sds(8 * N, NZ)] * 2,
        compiler_params=params(8),
        cost_estimate=cost(10**6, 11 * 2**20),
        name="boundary",
    )(freq_index, links, u, ab, w, rx0, rx1, ry0, ry1, rt0, rt1)

    forward = pl.pallas_call(
        field_kernel,
        grid=(steps,),
        in_specs=[whole()] * 3,
        out_specs=block3(6),
        out_shape=sds(6, CELLS, NZ),
        compiler_params=params(6),
        cost_estimate=cost(10**6, 6 * 2**20),
        name="field",
    )(w, planes, rows)

    mine_b = keep_b + swap_freq(send_b, 1)
    partner_b, partner, forward = lax.optimization_barrier((swap_freq(mine_b, 2), partner, forward))
    mine = mine + partner
    mine_b = mine_b + partner_b
    other = swap_freq(mine, 1)
    other_b = swap_freq(mine_b, 1)

    grad_h, grad_v = pl.pallas_call(
        gradient_kernel,
        grid=(steps,),
        in_specs=[block2, block2, whole(), whole(), whole(), block2, block2],
        out_specs=[block2, block2],
        out_shape=[sds(CELLS, NZ)] * 2,
        scratch_shapes=[pltpu.VMEM((BLOCK, NZ), f32)],
        compiler_params=params(6),
        cost_estimate=cost(10**6, 4 * 2**20),
        name="gradient",
    )(mine, other, mine_b, other_b, ab, cond_h, cond_v)

    return (
        forward.reshape(1, 1, 2, 3, N, N, NZ),
        grad_h.reshape(1, N, N, NZ),
        grad_v.reshape(1, N, N, NZ),
    )


def solution(mesh):
    return jax.shard_map(
        on_device,
        mesh=mesh,
        in_specs=(
            P("sub", None, None, None, None, None),
            P("freq", "sub", None, None, None, None, None),
            P("sub", None, None, None),
            P("sub", None, None, None),
            P("sub", None, None),
            P("sub", None),
            P("freq"),
        ),
        out_specs=(
            P("freq", "sub", None, None, None, None, None),
            P("sub", None, None, None),
            P("sub", None, None, None),
        ),
        check_vma=False,
    )
```

```python
import jax
import jax.numpy as jnp
from jax import lax
from jax.experimental import pallas as pl
from jax.experimental.pallas import tpu as pltpu
from jax.sharding import PartitionSpec as P

SX = 8
SUBS = 64
N = 32
NZ = 128
PIECES = (20, 8)
INNER = N - 4
PLANE = 40
ROWS = 34 * PLANE
STEP = 8
BLOCK = STEP * N
CELLS = N * N
NF = 12
FACE = NF * N
X_S, X_R, X_C, X_ROWS = 2 * FACE, 2 * FACE + 64, 2 * FACE + 112, 2 * FACE + 120
Y_ROWS = 2 * FACE + 64
T_ROWS = 72

P_ROBIN = 0.25
OMEGA0 = 0.5
KEEP = 1.0 + P_ROBIN
f32 = jnp.float32


def whole(space=pltpu.VMEM):
    return pl.BlockSpec(memory_space=space)


def params(mib):
    return pltpu.CompilerParams(vmem_limit_bytes=mib * 2**20)


def in_hbm(value):
    return pltpu.with_memory_space_constraint(value, pltpu.HBM)


def cost(flops, size):
    return pl.CostEstimate(flops=flops, bytes_accessed=size, transcendentals=0)


def base(x):
    return (x + 1) * PLANE


def scale_of(freq_ref):
    return OMEGA0 * jnp.left_shift(jnp.int32(1), freq_ref[0]).astype(f32)


def link_of(links_ref, k):
    return links_ref[0:1, k:k + 1].astype(f32)


def lane_neighbours(u):
    lane = lax.broadcasted_iota(jnp.int32, u.shape, 1)
    before = jnp.where(lane == 0, 0.0, pltpu.roll(u, 1, 1))
    after = jnp.where(lane == NZ - 1, 0.0, pltpu.roll(u, NZ - 1, 1))
    return before + after


def row_neighbours(u):
    row = lax.broadcasted_iota(jnp.int32, u.shape, 0)
    before = jnp.where(row == 0, 0.0, pltpu.roll(u, 1, 0))
    after = jnp.where(row == N - 1, 0.0, pltpu.roll(u, N - 1, 0))
    return before + after


def factors(shift):
    inverse = 1.0 / (36.0 + shift * shift)
    return jnp.where(shift > 0.0, 6.0 * inverse, 0.0), shift * inverse


def times(ab, re, im):
    a, b = ab
    return a * re + b * im, a * im - b * re


def pairs():
    for solve in range(2):
        for comp in range(3):
            yield solve * 6 + comp, solve * 6 + 3 + comp, comp // 2


def trace(outer, inner):
    return KEEP * outer - P_ROBIN * inner


def stencil(ref, f, x):
    start = base(x)
    centre = ref[f, pl.ds(start, N), :]
    total = ref[f, pl.ds(start - PLANE, N), :] + ref[f, pl.ds(start + PLANE, N), :]
    total = total + (ref[f, pl.ds(start - 1, N), :] + ref[f, pl.ds(start + 1, N), :])
    return total + lane_neighbours(centre)


def floor_column(floor_ref, x, first, size):
    floor = floor_ref[pl.ds(x, 1), :].astype(f32)
    row = lax.broadcasted_iota(jnp.int32, (size, N), 0) + first
    col = lax.broadcasted_iota(jnp.int32, (size, N), 1)
    return jnp.sum(jnp.where(row == col, floor, 0.0), axis=1, keepdims=True)


def mask_of(column):
    depth = lax.broadcasted_iota(jnp.int32, (column.shape[0], NZ), 1).astype(f32)
    return (depth >= column).astype(f32)


def parity():
    sub = lax.axis_index("sub")
    return lax.rem(sub, 2) == 1, lax.rem(lax.div(sub, SX), 2) == 1


def face(out_ref, shift, field, keep=None):
    ab = [[factors(value) for value in layer] for layer in shift]
    for k in range(2):
        out_ref[X_S + k * N:X_S + (k + 1) * N, :] = shift[0][k]
    for fr, fi, k in pairs():
        u = [times(ab[l][k], field(fr, l), field(fi, l)) for l in range(3)]
        v = []
        for l in range(2):
            near = [u[l + 1][c] if l == 0 else u[0][c] + u[2][c] for c in range(2)]
            total = [near[c] + row_neighbours(u[l][c]) + lane_neighbours(u[l][c]) for c in range(2)]
            new = times(ab[l][k], *total)
            v.append([u[l][c] + new[c] for c in range(2)])
        for c, f in enumerate((fr, fi)):
            out_ref[f * N:(f + 1) * N, :] = trace(u[0][c], u[1][c])
            out_ref[FACE + f * N:FACE + (f + 1) * N, :] = trace(v[0][c], v[1][c])
            if keep is not None:
                keep(f, u[0][c], u[1][c])


def strip_kernel(
    freq_ref, links_ref, floor_ref,
    srcx_ref, adjx_ref, shx_ref, svx_ref, srcy_ref, adjy_ref, shy_ref, svy_ref,
    px0_ref, px1_ref, py0_ref, py1_ref, xl_ref, xh_ref, yl_ref, yh_ref,
):
    step = pl.program_id(0)
    scale = scale_of(freq_ref)
    odd_x, odd_y = parity()
    fields = [ref.reshape(6, N * 8, NZ) for ref in (srcy_ref, adjy_ref)]
    sigmas = [ref.reshape(N * 8, NZ) for ref in (shy_ref, svy_ref)]

    def side(s, x_ref, y_ref):
        def plane(l):
            return slice((3 - l) * N, (4 - l) * N) if s else slice(l * N, (l + 1) * N)

        def line(l):
            return pl.ds(7 - l if s else l, N, stride=8)

        def field_x(f, l):
            return srcx_ref[f, plane(l), :] if f < 6 else adjx_ref[f - 6, plane(l), :]

        def field_y(f, l):
            return fields[f // 6][f % 6, line(l), :]

        def relay(f, outer, inner):
            for e in range(2):
                for l, value in enumerate((outer, inner)):
                    at = X_R + e * 24 + f * 2 + l
                    row = [value[y:y + 1, :] for y in ((N - 1, N - 2) if e else (0, 1))]
                    x_ref[at:at + 1, :] = link_of(links_ref, 2 + e) * trace(*row)

        layers = [N - 1 - l if s else l for l in range(3)]
        masks = [mask_of(floor_column(floor_ref, x, 0, N)) for x in layers]
        shift = [[scale * ref[plane(l), :] * masks[l] for ref in (shx_ref, svx_ref)] for l in range(3)]
        face(x_ref, shift, field_x, relay)
        for end in range(2):
            for k in range(2):
                for l in range(2):
                    at = X_C + end * 4 + k * 2 + l
                    x_ref[at:at + 1, :] = shift[l][k][end * (N - 1):end * (N - 1) + 1, :]
        masks = [mask_of(floor_ref[:, y:y + 1].astype(f32)) for y in layers]
        shift = [[scale * ref[line(l), :] * masks[l] for ref in sigmas] for l in range(3)]
        face(y_ref, shift, field_y)

    @pl.when(step == 0)
    def _():
        side(0, xl_ref, yl_ref)

    @pl.when(step == 1)
    def _():
        side(1, xh_ref, yh_ref)
        low, high = xl_ref[...], xh_ref[...]
        px0_ref[...] = jnp.where(odd_x, low, high)
        px1_ref[...] = jnp.where(odd_x, high, low)
        low, high = yl_ref[...], yh_ref[...]
        py0_ref[...] = jnp.where(odd_y, low, high)
        py1_ref[...] = jnp.where(odd_y, high, low)


def edge_kernel(links_ref, ab_ref, rx0_ref, rx1_ref, ty0_ref, ty1_ref, tl_ref, th_ref):
    odd_x, odd_y = parity()

    def from_x(side, rows):
        first, second = rx0_ref[rows, :], rx1_ref[rows, :]
        return jnp.where(odd_x, first, second) if side == 0 else jnp.where(odd_x, second, first)

    for e, t_ref in enumerate((tl_ref, th_ref)):
        outer, inner = (0, 1) if e == 0 else (N - 1, N - 2)
        for side in range(2):
            link = link_of(links_ref, side)
            x = side * (N - 1)
            for fr, fi, k in pairs():
                layers = []
                for y in (outer, inner):
                    at = x * N + y
                    ab = (ab_ref[2 * k, at:at + 1, :], ab_ref[2 * k + 1, at:at + 1, :])
                    re = link * from_x(side, slice(fr * N + y, fr * N + y + 1))
                    im = link * from_x(side, slice(fi * N + y, fi * N + y + 1))
                    layers.append(times(ab, re, im))
                t_ref[side * NF + fr:side * NF + fr + 1, :] = trace(layers[0][0], layers[1][0])
                t_ref[side * NF + fi:side * NF + fi + 1, :] = trace(layers[0][1], layers[1][1])
            at = X_R + e * 24
            t_ref[24 + side * 24:48 + side * 24, :] = from_x(side, slice(at, at + 24))
    low, high = tl_ref[...], th_ref[...]
    ty0_ref[...] = jnp.where(odd_y, low, high)
    ty1_ref[...] = jnp.where(odd_y, high, low)


def solve_kernel(
    freq_ref, floor_ref, src_ref, adj_ref, sh_ref, sv_ref,
    u_ref, ab_ref, w_ref, *refs,
):
    step = pl.program_id(0)
    scale = scale_of(freq_ref)
    odd_core = lax.rem(lax.axis_index("freq"), 2) == 1
    count = len(PIECES)
    keep_refs, send_refs, v_ref = refs[:count], refs[count:2 * count], refs[2 * count]

    @pl.when(step == 0)
    def _():
        zeros = jnp.zeros((PLANE, NZ), f32)
        for f in range(NF):
            for ref in (u_ref, v_ref):
                ref[f, 0:PLANE, :] = zeros
                ref[f, ROWS - PLANE:ROWS, :] = zeros

    @pl.when(step < N // STEP)
    def _():
        def plane(j, carry):
            x = step * STEP + j
            here = pl.ds(pl.multiple_of(j * N, N), N)
            there = pl.ds(pl.multiple_of(x * N, N), N)
            start = pl.multiple_of(base(x), 8)
            mask = mask_of(floor_column(floor_ref, x, 0, N))
            ab = []
            for k, ref in enumerate((sh_ref, sv_ref)):
                ab.append(factors(scale * ref[here, :] * mask))
                ab_ref[2 * k, there, :] = ab[k][0]
                ab_ref[2 * k + 1, there, :] = ab[k][1]
            zeros = jnp.zeros((8, NZ), f32)
            for fr, fi, k in pairs():
                ref, g = (src_ref, 0) if fr < 6 else (adj_ref, 6)
                re, im = times(ab[k], ref[fr - g, here, :], ref[fi - g, here, :])
                for f, value in ((fr, re), (fi, im)):
                    u_ref[f, pl.ds(start, N), :] = value
                    u_ref[f, pl.ds(start + N, 8), :] = zeros
                    v_ref[f, pl.ds(start + N, 8), :] = zeros
            return carry

        lax.fori_loop(0, STEP, plane, 0, unroll=4)

    @pl.when(step > 0)
    def _():
        def plane(j, carry):
            x = (step - 1) * STEP + j
            there = pl.ds(pl.multiple_of(x * N, N), N)
            start = pl.multiple_of(base(x), 8)
            ab = [(ab_ref[2 * k, there, :], ab_ref[2 * k + 1, there, :]) for k in range(2)]
            for fr, fi, k in pairs():
                re, im = times(ab[k], stencil(u_ref, fr, x), stencil(u_ref, fi, x))
                v_ref[fr, pl.ds(start, N), :] = u_ref[fr, pl.ds(start, N), :] + re
                v_ref[fi, pl.ds(start, N), :] = u_ref[fi, pl.ds(start, N), :] + im
            return carry

        lax.fori_loop(0, STEP, plane, 0, unroll=4)

    @pl.when(step == N // STEP)
    def _():
        def last_update(x):
            there = pl.ds(pl.multiple_of(x * N, N), N)
            start = pl.multiple_of(base(x), 8)
            ab = [(ab_ref[2 * k, there, :], ab_ref[2 * k + 1, there, :]) for k in range(2)]
            term = [None, None]
            for comp in range(3):
                k = comp // 2
                new = []
                for solve in range(2):
                    fr, fi = solve * 6 + comp, solve * 6 + 3 + comp
                    re, im = times(ab[k], stencil(v_ref, fr, x), stencil(v_ref, fi, x))
                    re = re + u_ref[fr, pl.ds(start, N), :]
                    im = im + u_ref[fi, pl.ds(start, N), :]
                    w_ref[fr, there, :] = re
                    w_ref[fi, there, :] = im
                    new.append((re, im))
                product = new[1][0] * new[0][1] + new[1][1] * new[0][0]
                term[k] = product if term[k] is None else term[k] + product
            return term

        for x in (0, 1, N - 2, N - 1):
            last_update(x)
        first = 2
        for size, keep_ref, send_ref in zip(PIECES, keep_refs, send_refs):
            def plane(j, carry, first=first, keep_ref=keep_ref, send_ref=send_ref):
                here = pl.ds(j * INNER, INNER)
                term = last_update(first + j)
                term_h, term_v = scale * term[0], scale * term[1]
                keep_ref[here, :] = jnp.where(odd_core, term_v, term_h)[2:N - 2, :]
                send_ref[here, :] = jnp.where(odd_core, term_h, term_v)[2:N - 2, :]
                return carry

            lax.fori_loop(0, size, plane, 0, unroll=2)
            first += size


def boundary_kernel(
    freq_ref, links_ref, u_ref, ab_ref, w_ref, rx0_ref, rx1_ref, ry0_ref, ry1_ref, rt0_ref, rt1_ref,
    planes_ref, rows_ref, keep_ref, send_ref,
):
    scale = scale_of(freq_ref)
    odd_x, odd_y = parity()
    odd_core = lax.rem(lax.axis_index("freq"), 2) == 1
    link = [link_of(links_ref, k) for k in range(4)]
    row = lax.broadcasted_iota(jnp.int32, (N, NZ), 0)

    def pick(odd, side, first_ref, second_ref, rows):
        first, second = first_ref[rows, :], second_ref[rows, :]
        return jnp.where(odd, first, second) if side == 0 else jnp.where(odd, second, first)

    def from_x(side, at, size):
        return pick(odd_x, side, rx0_ref, rx1_ref, slice(at, at + size))

    def from_y(side, at, size):
        return pick(odd_y, side, ry0_ref, ry1_ref, slice(at, at + size))

    def from_t(side, at, size):
        return pick(odd_y, side, rt0_ref, rt1_ref, slice(at, at + size))

    def ends(first, last):
        return jnp.where(row == 0, first, jnp.where(row == N - 1, last, 0.0))

    def ab_plane(k, x):
        return ab_ref[2 * k, x * N:(x + 1) * N, :], ab_ref[2 * k + 1, x * N:(x + 1) * N, :]

    def ab_row(k, y):
        return ab_ref[2 * k, pl.ds(y, N, stride=N), :], ab_ref[2 * k + 1, pl.ds(y, N, stride=N), :]

    near_x = [[factors(from_x(s, X_S + k * N, N)) for k in range(2)] for s in range(2)]
    near_y = [[factors(from_y(s, X_S + k * N, N)) for k in range(2)] for s in range(2)]
    corner = [[[[factors(from_x(s, X_C + e * 4 + k * 2 + layer, 1)) for layer in range(2)]
                for k in range(2)] for e in range(2)] for s in range(2)]

    for fr, fi, k in pairs():
        both = (fr, fi)
        edge, ghost_y = [], []
        for e in range(2):
            outer, inner = (0, 1) if e == 0 else (N - 1, N - 2)
            g1 = [link[2 + e] * from_y(e, f * N, N) for f in both]
            edge.append((g1, times(ab_row(k, outer), *g1)))
            own = [trace(u_ref[f, pl.ds(base(0) + outer, N, stride=PLANE), :],
                         u_ref[f, pl.ds(base(0) + inner, N, stride=PLANE), :]) for f in both]
            back = times(near_y[e][k], *own)
            ghost_y.append([
                link[2 + e] * (from_y(e, FACE + f * N, N) + KEEP * back[c] + ends(from_t(e, f, 1), from_t(e, NF + f, 1)))
                for c, f in enumerate(both)
            ])
        for s in range(2):
            x0, x1, x2 = (0, 1, 2) if s == 0 else (N - 1, N - 2, N - 3)
            g1 = [link[s] * from_x(s, f * N, N) + ends(edge[0][0][c][x0:x0 + 1, :], edge[1][0][c][x0:x0 + 1, :])
                  for c, f in enumerate(both)]
            ab0, ab1 = ab_plane(k, x0), ab_plane(k, x1)
            w0 = times(ab0, *g1)
            own = [trace(u_ref[f, base(x0):base(x0) + N, :], u_ref[f, base(x1):base(x1) + N, :]) for f in both]
            back = times(near_x[s][k], *own)
            corners = []
            for e in range(2):
                layers = []
                for layer in range(2):
                    relay = [from_t(e, 24 + s * 24 + f * 2 + layer, 1) for f in both]
                    layers.append(times(corner[s][e][k][layer], *relay))
                corners.append([trace(layers[0][c], layers[1][c]) for c in range(2)])
            rhs0, rhs1 = [], []
            for c, f in enumerate(both):
                ghost = link[s] * (from_x(s, FACE + f * N, N) + KEEP * back[c] + ends(corners[0][c], corners[1][c]))
                m1 = ends(edge[0][1][c][x1:x1 + 1, :], edge[1][1][c][x1:x1 + 1, :])
                m2 = ends(edge[0][1][c][x2:x2 + 1, :], edge[1][1][c][x2:x2 + 1, :])
                side0 = ends(ghost_y[0][c][x0:x0 + 1, :], ghost_y[1][c][x0:x0 + 1, :])
                side1 = ends(ghost_y[0][c][x1:x1 + 1, :], ghost_y[1][c][x1:x1 + 1, :])
                rhs0.append(row_neighbours(w0[c]) + lane_neighbours(w0[c]) + m1 + ghost + side0)
                rhs1.append(w0[c] + m2 + row_neighbours(m1) + lane_neighbours(m1) + side1)
            fix0, fix1 = times(ab0, *rhs0), times(ab1, *rhs1)
            at0, at1 = (0, 1) if s == 0 else (3, 2)
            for c, f in enumerate(both):
                planes_ref[f, at0 * N:(at0 + 1) * N, :] = w_ref[f, x0 * N:(x0 + 1) * N, :] + fix0[c]
                planes_ref[f, at1 * N:(at1 + 1) * N, :] = w_ref[f, x1 * N:(x1 + 1) * N, :] + fix1[c]
        for e in range(2):
            outer, inner = (0, 1) if e == 0 else (N - 1, N - 2)
            w0 = edge[e][1]
            rhs = [row_neighbours(w0[c]) + lane_neighbours(w0[c]) + ghost_y[e][c] for c in range(2)]
            fix0 = times(ab_row(k, outer), *rhs)
            fix1 = times(ab_row(k, inner), *w0)
            at0, at1 = (0, 1) if e == 0 else (3, 2)
            for c, f in enumerate(both):
                rows_ref[f, at0 * N:(at0 + 1) * N, :] = w_ref[f, pl.ds(outer, N, stride=N), :] + fix0[c]
                rows_ref[f, at1 * N:(at1 + 1) * N, :] = w_ref[f, pl.ds(inner, N, stride=N), :] + fix1[c]
    for ref, at in ((planes_ref, 0), (rows_ref, 4 * N)):
        term = [None, None]
        for comp in range(3):
            product = ref[6 + comp] * ref[3 + comp] + ref[9 + comp] * ref[comp]
            term[comp // 2] = product if comp % 2 == 0 else term[0] + product
        term_h, term_v = scale * term[0], scale * term[1]
        keep_ref[at:at + 4 * N, :] = jnp.where(odd_core, term_v, term_h)
        send_ref[at:at + 4 * N, :] = jnp.where(odd_core, term_h, term_v)


def put_boundary(step, block_ref, index, planes, rows):
    for at, y in enumerate((0, 1, N - 2, N - 1)):
        block_ref[(*index, pl.ds(y, STEP, stride=N), slice(None))] = rows(at)

    @pl.when(step == 0)
    def _():
        block_ref[(*index, slice(0, 2 * N), slice(None))] = planes(0)

    @pl.when(step == N // STEP - 1)
    def _():
        block_ref[(*index, slice(BLOCK - 2 * N, BLOCK), slice(None))] = planes(2 * N)


def field_kernel(w_ref, planes_ref, rows_ref, out_ref):
    step = pl.program_id(0)
    out_ref[...] = w_ref[0:6, pl.ds(pl.multiple_of(step * BLOCK, BLOCK), BLOCK), :]
    for f in range(6):
        put_boundary(
            step, out_ref, (f,),
            lambda at, f=f: planes_ref[f, at:at + 2 * N, :],
            lambda at, f=f: rows_ref[f, pl.ds(pl.multiple_of(at * N + step * STEP, 8), STEP), :],
        )


def gradient_kernel(mine_ref, other_ref, mine_b_ref, other_b_ref, ab_ref, sh_ref, sv_ref, gh_ref, gv_ref, total_ref):
    step = pl.program_id(0)
    odd_core = lax.rem(lax.axis_index("freq"), 2) == 1
    mask = (ab_ref[0, pl.ds(pl.multiple_of(step * BLOCK, BLOCK), BLOCK), :] > 0.0).astype(f32)
    for k, (sigma_ref, out_ref) in enumerate(((sh_ref, gh_ref), (sv_ref, gv_ref))):
        first = odd_core if k == 1 else jnp.logical_not(odd_core)
        for j in range(STEP):
            inner = jnp.clip(step * STEP + j - 2, 0, INNER - 1)
            rows = pl.ds(inner * INNER, INNER)
            total_ref[j * N + 2:(j + 1) * N - 2, :] = jnp.where(first, mine_ref[rows, :], other_ref[rows, :])

        def boundary(rows):
            return jnp.where(first, mine_b_ref[rows, :], other_b_ref[rows, :])

        put_boundary(
            step, total_ref, (),
            lambda at: boundary(slice(at, at + 2 * N)),
            lambda at: boundary(pl.ds(pl.multiple_of((4 + at) * N + step * STEP, 8), STEP)),
        )
        out_ref[...] = sigma_ref[...] * mask * total_ref[...]


def swap_pairs(axis, odd):
    pairs_of = []
    for i in range(SUBS):
        at = [i % SX, i // SX]
        at[axis] += 1 if at[axis] % 2 == odd else -1
        if 0 <= at[axis] < SX:
            pairs_of.append((i, at[1] * SX + at[0]))
    return pairs_of


def swap(value, axis, odd):
    return lax.ppermute(value, "sub", swap_pairs(axis, odd))


def swap_freq(value, flip):
    return lax.ppermute(value, "freq", [(i, i ^ flip) for i in range(4)])


def sds(*shape):
    return jax.ShapeDtypeStruct(shape, f32)


def on_device(source, adjoint_source, sigma_h, sigma_v, seafloor, links, freq_index):
    steps = N // STEP
    src = in_hbm(source.reshape(6, N, N, NZ))
    adj = in_hbm(adjoint_source.reshape(6, N, N, NZ))
    cond_h = sigma_h.reshape(CELLS, NZ)
    cond_v = sigma_v.reshape(CELLS, NZ)
    cond_h4 = in_hbm(sigma_h.reshape(N, N, NZ))
    cond_v4 = in_hbm(sigma_v.reshape(N, N, NZ))
    floor = in_hbm(seafloor.reshape(N, N))
    links = in_hbm(links)
    smem = whole(pltpu.SMEM)

    def block3(size):
        return pl.BlockSpec((size, BLOCK, NZ), lambda i: (0, jnp.minimum(i, steps - 1), 0))

    block2 = pl.BlockSpec((BLOCK, NZ), lambda i: (jnp.minimum(i, steps - 1), 0))

    flat_src, flat_adj = in_hbm(source.reshape(6, CELLS, NZ)), in_hbm(adjoint_source.reshape(6, CELLS, NZ))
    flat_h, flat_v = in_hbm(cond_h), in_hbm(cond_v)
    last = N // 4 - 1
    field_x = pl.BlockSpec((6, 4 * N, NZ), lambda i: (0, i * last, 0))
    sigma_x = pl.BlockSpec((4 * N, NZ), lambda i: (i * last, 0))
    field_y = pl.BlockSpec((6, N, 8, NZ), lambda i: (0, 0, i * (N // 8 - 1), 0))
    sigma_y = pl.BlockSpec((N, 8, NZ), lambda i: (0, i * (N // 8 - 1), 0))
    px0, px1, py0, py1 = pl.pallas_call(
        strip_kernel,
        grid=(2,),
        in_specs=[smem] + [whole()] * 2 + [field_x, field_x, sigma_x, sigma_x, field_y, field_y, sigma_y, sigma_y],
        out_specs=[whole()] * 4,
        out_shape=[sds(X_ROWS, NZ), sds(X_ROWS, NZ), sds(Y_ROWS, NZ), sds(Y_ROWS, NZ)],
        scratch_shapes=[pltpu.VMEM((X_ROWS, NZ), f32)] * 2 + [pltpu.VMEM((Y_ROWS, NZ), f32)] * 2,
        compiler_params=params(14),
        cost_estimate=cost(10**6, 12 * 2**20),
        name="strips",
    )(freq_index, links, floor, flat_src, flat_adj, flat_h, flat_v, src, adj, cond_h4, cond_v4)
    ry1 = swap(py1, 1, 1)
    ry0 = swap(py0, 1, 0)
    rx1 = swap(px1, 0, 1)
    rx0 = swap(px0, 0, 0)

    u, ab, w, *terms = pl.pallas_call(
        solve_kernel,
        grid=(steps + 1,),
        in_specs=[smem, whole(), block3(6), block3(6), block2, block2],
        out_specs=[whole()] * (3 + 2 * len(PIECES)),
        out_shape=[
            pltpu.VMEM((NF, ROWS, NZ), f32), pltpu.VMEM((4, CELLS, NZ), f32), pltpu.VMEM((NF, CELLS, NZ), f32),
        ] + [sds(size * INNER, NZ) for size in PIECES] * 2,
        scratch_shapes=[pltpu.VMEM((NF, ROWS, NZ), f32)],
        compiler_params=params(16),
        cost_estimate=cost(60 * NF * CELLS * NZ, 40 * 2**20),
        name="solve",
    )(freq_index, floor, flat_src, flat_adj, flat_h, flat_v)

    ty0, ty1 = pl.pallas_call(
        edge_kernel,
        in_specs=[whole()] * 4,
        out_specs=[whole()] * 2,
        out_shape=[sds(T_ROWS, NZ)] * 2,
        scratch_shapes=[pltpu.VMEM((T_ROWS, NZ), f32)] * 2,
        compiler_params=params(4),
        cost_estimate=cost(1000, 1000),
        name="edges",
    )(links, ab, rx0, rx1)
    rt1 = swap(ty1, 1, 1)
    rt0 = swap(ty0, 1, 0)

    part = [keep + swap_freq(send, 1) for keep, send in zip(terms[:len(PIECES)], terms[len(PIECES):])]
    partner = [swap_freq(value, 2) for value in part]

    planes, rows, keep_b, send_b = pl.pallas_call(
        boundary_kernel,
        in_specs=[smem] + [whole()] * 10,
        out_specs=[whole()] * 4,
        out_shape=[pltpu.VMEM((NF, 4 * N, NZ), f32)] * 2 + [sds(8 * N, NZ)] * 2,
        compiler_params=params(8),
        cost_estimate=cost(1000, 1000),
        name="boundary",
    )(freq_index, links, u, ab, w, rx0, rx1, ry0, ry1, rt0, rt1)

    forward = pl.pallas_call(
        field_kernel,
        grid=(steps,),
        in_specs=[whole()] * 3,
        out_specs=block3(6),
        out_shape=sds(6, CELLS, NZ),
        compiler_params=params(6),
        cost_estimate=cost(1000, 1000),
        name="field",
    )(w, planes, rows)

    mine_b = keep_b + swap_freq(send_b, 1)
    partner_b, partner, forward = lax.optimization_barrier((swap_freq(mine_b, 2), partner, forward))
    mine = jnp.concatenate([value + other for value, other in zip(part, partner)], axis=0)
    mine_b = mine_b + partner_b
    other = swap_freq(mine, 1)
    other_b = swap_freq(mine_b, 1)

    grad_h, grad_v = pl.pallas_call(
        gradient_kernel,
        grid=(steps,),
        in_specs=[whole()] * 5 + [block2, block2],
        out_specs=[block2, block2],
        out_shape=[sds(CELLS, NZ)] * 2,
        scratch_shapes=[pltpu.VMEM((BLOCK, NZ), f32)],
        compiler_params=params(6),
        cost_estimate=cost(1000, 1000),
        name="gradient",
    )(mine, other, mine_b, other_b, ab, cond_h, cond_v)

    return (
        forward.reshape(1, 1, 2, 3, N, N, NZ),
        grad_h.reshape(1, N, N, NZ),
        grad_v.reshape(1, N, N, NZ),
    )


def solution(mesh):
    return jax.shard_map(
        on_device,
        mesh=mesh,
        in_specs=(
            P("sub", None, None, None, None, None),
            P("freq", "sub", None, None, None, None, None),
            P("sub", None, None, None),
            P("sub", None, None, None),
            P("sub", None, None),
            P("sub", None),
            P("freq"),
        ),
        out_specs=(
            P("freq", "sub", None, None, None, None, None),
            P("sub", None, None, None),
            P("sub", None, None, None),
        ),
        check_vma=False,
    )
```

```python
import jax
import jax.numpy as jnp
from jax import lax
from jax.experimental import pallas as pl
from jax.experimental.pallas import tpu as pltpu
from jax.sharding import PartitionSpec as P

SX = 8
SUBS = 64
N = 32
NZ = 128
PIECES = (25, 3)
INNER = N - 4
PLANE = 40
ROWS = 34 * PLANE
STEP = 8
BLOCK = STEP * N
CELLS = N * N
NF = 12
FACE = NF * N
X_S, X_R, X_C, X_ROWS = 2 * FACE, 2 * FACE + 64, 2 * FACE + 112, 2 * FACE + 120
Y_ROWS = 2 * FACE + 64
T_ROWS = 72

P_ROBIN = 0.25
OMEGA0 = 0.5
KEEP = 1.0 + P_ROBIN
f32 = jnp.float32


def whole(space=pltpu.VMEM):
    return pl.BlockSpec(memory_space=space)


def params(mib):
    return pltpu.CompilerParams(vmem_limit_bytes=mib * 2**20)


def in_hbm(value):
    return pltpu.with_memory_space_constraint(value, pltpu.HBM)


def cost(flops, size):
    return pl.CostEstimate(flops=flops, bytes_accessed=size, transcendentals=0)


def base(x):
    return (x + 1) * PLANE


def scale_of(freq_ref):
    return OMEGA0 * jnp.left_shift(jnp.int32(1), freq_ref[0]).astype(f32)


def link_of(links_ref, k):
    return links_ref[0:1, k:k + 1].astype(f32)


def lane_neighbours(u):
    lane = lax.broadcasted_iota(jnp.int32, u.shape, 1)
    before = jnp.where(lane == 0, 0.0, pltpu.roll(u, 1, 1))
    after = jnp.where(lane == NZ - 1, 0.0, pltpu.roll(u, NZ - 1, 1))
    return before + after


def row_neighbours(u):
    row = lax.broadcasted_iota(jnp.int32, u.shape, 0)
    before = jnp.where(row == 0, 0.0, pltpu.roll(u, 1, 0))
    after = jnp.where(row == N - 1, 0.0, pltpu.roll(u, N - 1, 0))
    return before + after


def factors(shift):
    inverse = 1.0 / (36.0 + shift * shift)
    return jnp.where(shift > 0.0, 6.0 * inverse, 0.0), shift * inverse


def times(ab, re, im):
    a, b = ab
    return a * re + b * im, a * im - b * re


def pairs():
    for solve in range(2):
        for comp in range(3):
            yield solve * 6 + comp, solve * 6 + 3 + comp, comp // 2


def trace(outer, inner):
    return KEEP * outer - P_ROBIN * inner


def stencil(ref, f, x):
    start = base(x)
    centre = ref[f, pl.ds(start, N), :]
    total = ref[f, pl.ds(start - PLANE, N), :] + ref[f, pl.ds(start + PLANE, N), :]
    total = total + (ref[f, pl.ds(start - 1, N), :] + ref[f, pl.ds(start + 1, N), :])
    return total + lane_neighbours(centre)


def floor_column(floor_ref, x, first, size):
    floor = floor_ref[pl.ds(x, 1), :].astype(f32)
    row = lax.broadcasted_iota(jnp.int32, (size, N), 0) + first
    col = lax.broadcasted_iota(jnp.int32, (size, N), 1)
    return jnp.sum(jnp.where(row == col, floor, 0.0), axis=1, keepdims=True)


def mask_of(column):
    depth = lax.broadcasted_iota(jnp.int32, (column.shape[0], NZ), 1).astype(f32)
    return (depth >= column).astype(f32)


def parity():
    sub = lax.axis_index("sub")
    return lax.rem(sub, 2) == 1, lax.rem(lax.div(sub, SX), 2) == 1


def face(out_ref, shift, field, keep=None):
    ab = [[factors(value) for value in layer] for layer in shift]
    for k in range(2):
        out_ref[X_S + k * N:X_S + (k + 1) * N, :] = shift[0][k]
    for fr, fi, k in pairs():
        u = [times(ab[l][k], field(fr, l), field(fi, l)) for l in range(3)]
        v = []
        for l in range(2):
            near = [u[l + 1][c] if l == 0 else u[0][c] + u[2][c] for c in range(2)]
            total = [near[c] + row_neighbours(u[l][c]) + lane_neighbours(u[l][c]) for c in range(2)]
            new = times(ab[l][k], *total)
            v.append([u[l][c] + new[c] for c in range(2)])
        for c, f in enumerate((fr, fi)):
            out_ref[f * N:(f + 1) * N, :] = trace(u[0][c], u[1][c])
            out_ref[FACE + f * N:FACE + (f + 1) * N, :] = trace(v[0][c], v[1][c])
            if keep is not None:
                keep(f, u[0][c], u[1][c])


def strip_kernel(
    freq_ref, links_ref, floor_ref,
    srcx_ref, adjx_ref, shx_ref, svx_ref, srcy_ref, adjy_ref, shy_ref, svy_ref,
    px0_ref, px1_ref, py0_ref, py1_ref, xl_ref, xh_ref, yl_ref, yh_ref,
):
    step = pl.program_id(0)
    scale = scale_of(freq_ref)
    odd_x, odd_y = parity()
    fields = [ref.reshape(6, N * 8, NZ) for ref in (srcy_ref, adjy_ref)]
    sigmas = [ref.reshape(N * 8, NZ) for ref in (shy_ref, svy_ref)]

    def side(s, x_ref, y_ref):
        def plane(l):
            return slice((3 - l) * N, (4 - l) * N) if s else slice(l * N, (l + 1) * N)

        def line(l):
            return pl.ds(7 - l if s else l, N, stride=8)

        def field_x(f, l):
            return srcx_ref[f, plane(l), :] if f < 6 else adjx_ref[f - 6, plane(l), :]

        def field_y(f, l):
            return fields[f // 6][f % 6, line(l), :]

        def relay(f, outer, inner):
            for e in range(2):
                for l, value in enumerate((outer, inner)):
                    at = X_R + e * 24 + f * 2 + l
                    row = [value[y:y + 1, :] for y in ((N - 1, N - 2) if e else (0, 1))]
                    x_ref[at:at + 1, :] = link_of(links_ref, 2 + e) * trace(*row)

        layers = [N - 1 - l if s else l for l in range(3)]
        masks = [mask_of(floor_column(floor_ref, x, 0, N)) for x in layers]
        shift = [[scale * ref[plane(l), :] * masks[l] for ref in (shx_ref, svx_ref)] for l in range(3)]
        face(x_ref, shift, field_x, relay)
        for end in range(2):
            for k in range(2):
                for l in range(2):
                    at = X_C + end * 4 + k * 2 + l
                    x_ref[at:at + 1, :] = shift[l][k][end * (N - 1):end * (N - 1) + 1, :]
        masks = [mask_of(floor_ref[:, y:y + 1].astype(f32)) for y in layers]
        shift = [[scale * ref[line(l), :] * masks[l] for ref in sigmas] for l in range(3)]
        face(y_ref, shift, field_y)

    @pl.when(step == 0)
    def _():
        side(0, xl_ref, yl_ref)

    @pl.when(step == 1)
    def _():
        side(1, xh_ref, yh_ref)
        low, high = xl_ref[...], xh_ref[...]
        px0_ref[...] = jnp.where(odd_x, low, high)
        px1_ref[...] = jnp.where(odd_x, high, low)
        low, high = yl_ref[...], yh_ref[...]
        py0_ref[...] = jnp.where(odd_y, low, high)
        py1_ref[...] = jnp.where(odd_y, high, low)


def edge_kernel(links_ref, ab_ref, rx0_ref, rx1_ref, ty0_ref, ty1_ref, tl_ref, th_ref):
    odd_x, odd_y = parity()

    def from_x(side, rows):
        first, second = rx0_ref[rows, :], rx1_ref[rows, :]
        return jnp.where(odd_x, first, second) if side == 0 else jnp.where(odd_x, second, first)

    for e, t_ref in enumerate((tl_ref, th_ref)):
        outer, inner = (0, 1) if e == 0 else (N - 1, N - 2)
        for side in range(2):
            link = link_of(links_ref, side)
            x = side * (N - 1)
            for fr, fi, k in pairs():
                layers = []
                for y in (outer, inner):
                    at = x * N + y
                    ab = (ab_ref[2 * k, at:at + 1, :], ab_ref[2 * k + 1, at:at + 1, :])
                    re = link * from_x(side, slice(fr * N + y, fr * N + y + 1))
                    im = link * from_x(side, slice(fi * N + y, fi * N + y + 1))
                    layers.append(times(ab, re, im))
                t_ref[side * NF + fr:side * NF + fr + 1, :] = trace(layers[0][0], layers[1][0])
                t_ref[side * NF + fi:side * NF + fi + 1, :] = trace(layers[0][1], layers[1][1])
            at = X_R + e * 24
            t_ref[24 + side * 24:48 + side * 24, :] = from_x(side, slice(at, at + 24))
    low, high = tl_ref[...], th_ref[...]
    ty0_ref[...] = jnp.where(odd_y, low, high)
    ty1_ref[...] = jnp.where(odd_y, high, low)


def solve_kernel(
    freq_ref, floor_ref, src_ref, adj_ref, sh_ref, sv_ref,
    u_ref, ab_ref, w_ref, *refs,
):
    scale = scale_of(freq_ref)
    odd_core = lax.rem(lax.axis_index("freq"), 2) == 1
    count = len(PIECES)
    keep_refs, send_refs, v_ref = refs[:count], refs[count:2 * count], refs[2 * count]
    zeros = jnp.zeros((PLANE, NZ), f32)
    for f in range(NF):
        for ref in (u_ref, v_ref):
            ref[f, 0:PLANE, :] = zeros
            ref[f, ROWS - PLANE:ROWS, :] = zeros

    def first_update(x, carry):
        there = pl.ds(pl.multiple_of(x * N, N), N)
        start = pl.multiple_of(base(x), 8)
        mask = mask_of(floor_column(floor_ref, x, 0, N))
        ab = []
        for k, ref in enumerate((sh_ref, sv_ref)):
            ab.append(factors(scale * ref[there, :] * mask))
            ab_ref[2 * k, there, :] = ab[k][0]
            ab_ref[2 * k + 1, there, :] = ab[k][1]
        zeros = jnp.zeros((8, NZ), f32)
        for fr, fi, k in pairs():
            ref, g = (src_ref, 0) if fr < 6 else (adj_ref, 6)
            re, im = times(ab[k], ref[fr - g, there, :], ref[fi - g, there, :])
            for f, value in ((fr, re), (fi, im)):
                u_ref[f, pl.ds(start, N), :] = value
                u_ref[f, pl.ds(start + N, 8), :] = zeros
                v_ref[f, pl.ds(start + N, 8), :] = zeros
        return carry

    lax.fori_loop(0, N, first_update, 0, unroll=4)

    def second_update(x, carry):
        there = pl.ds(pl.multiple_of(x * N, N), N)
        start = pl.multiple_of(base(x), 8)
        ab = [(ab_ref[2 * k, there, :], ab_ref[2 * k + 1, there, :]) for k in range(2)]
        for fr, fi, k in pairs():
            re, im = times(ab[k], stencil(u_ref, fr, x), stencil(u_ref, fi, x))
            v_ref[fr, pl.ds(start, N), :] = u_ref[fr, pl.ds(start, N), :] + re
            v_ref[fi, pl.ds(start, N), :] = u_ref[fi, pl.ds(start, N), :] + im
        return carry

    lax.fori_loop(0, N, second_update, 0, unroll=4)

    def last_update(x):
        there = pl.ds(pl.multiple_of(x * N, N), N)
        start = pl.multiple_of(base(x), 8)
        ab = [(ab_ref[2 * k, there, :], ab_ref[2 * k + 1, there, :]) for k in range(2)]
        term = [None, None]
        for comp in range(3):
            k = comp // 2
            new = []
            for solve in range(2):
                fr, fi = solve * 6 + comp, solve * 6 + 3 + comp
                re, im = times(ab[k], stencil(v_ref, fr, x), stencil(v_ref, fi, x))
                re = re + u_ref[fr, pl.ds(start, N), :]
                im = im + u_ref[fi, pl.ds(start, N), :]
                w_ref[fr, there, :] = re
                w_ref[fi, there, :] = im
                new.append((re, im))
            product = new[1][0] * new[0][1] + new[1][1] * new[0][0]
            term[k] = product if term[k] is None else term[k] + product
        return term

    for x in (0, 1, N - 2, N - 1):
        last_update(x)
    first = 2
    for size, keep_ref, send_ref in zip(PIECES, keep_refs, send_refs):
        def plane(j, carry, first=first, keep_ref=keep_ref, send_ref=send_ref):
            here = pl.ds(j * INNER, INNER)
            term = last_update(first + j)
            term_h, term_v = scale * term[0], scale * term[1]
            keep_ref[here, :] = jnp.where(odd_core, term_v, term_h)[2:N - 2, :]
            send_ref[here, :] = jnp.where(odd_core, term_h, term_v)[2:N - 2, :]
            return carry

        lax.fori_loop(0, size, plane, 0, unroll=4)
        first += size


def boundary_kernel(
    freq_ref, links_ref, u_ref, ab_ref, w_ref, py0_ref, py1_ref,
    rx0_ref, rx1_ref, ry0_ref, ry1_ref, rt0_ref, rt1_ref, keep_in_ref, send_in_ref,
    planes_ref, rows_ref, keep_ref, send_ref,
):
    scale = scale_of(freq_ref)
    odd_x, odd_y = parity()
    odd_core = lax.rem(lax.axis_index("freq"), 2) == 1
    link = [link_of(links_ref, k) for k in range(4)]
    row = lax.broadcasted_iota(jnp.int32, (N, NZ), 0)

    def pick(odd, side, first_ref, second_ref, rows):
        first, second = first_ref[rows, :], second_ref[rows, :]
        return jnp.where(odd, first, second) if side == 0 else jnp.where(odd, second, first)

    def from_x(side, at, size):
        return pick(odd_x, side, rx0_ref, rx1_ref, slice(at, at + size))

    def from_y(side, at, size):
        return pick(odd_y, side, ry0_ref, ry1_ref, slice(at, at + size))

    def from_t(side, at, size):
        return pick(odd_y, side, rt0_ref, rt1_ref, slice(at, at + size))

    def ends(first, last):
        return jnp.where(row == 0, first, jnp.where(row == N - 1, last, 0.0))

    def ab_plane(k, x):
        return ab_ref[2 * k, x * N:(x + 1) * N, :], ab_ref[2 * k + 1, x * N:(x + 1) * N, :]

    def ab_row(k, y):
        return ab_ref[2 * k, pl.ds(y, N, stride=N), :], ab_ref[2 * k + 1, pl.ds(y, N, stride=N), :]

    near_x = [[factors(from_x(s, X_S + k * N, N)) for k in range(2)] for s in range(2)]
    near_y = [[factors(from_y(s, X_S + k * N, N)) for k in range(2)] for s in range(2)]
    corner = [[[[factors(from_x(s, X_C + e * 4 + k * 2 + layer, 1)) for layer in range(2)]
                for k in range(2)] for e in range(2)] for s in range(2)]

    row_factors = [[[ab_row(k, y) for y in ys] for ys in ((0, 1), (N - 1, N - 2))] for k in range(2)]

    for fr, fi, k in pairs():
        both = (fr, fi)
        edge, ghost_y = [], []
        for e in range(2):
            g1 = [link[2 + e] * from_y(e, f * N, N) for f in both]
            edge.append((g1, times(row_factors[k][e][0], *g1)))
            own = [pick(odd_y, e, py0_ref, py1_ref, slice(f * N, (f + 1) * N)) for f in both]
            back = times(near_y[e][k], *own)
            ghost_y.append([
                link[2 + e] * (from_y(e, FACE + f * N, N) + KEEP * back[c] + ends(from_t(e, f, 1), from_t(e, NF + f, 1)))
                for c, f in enumerate(both)
            ])
        for s in range(2):
            x0, x1, x2 = (0, 1, 2) if s == 0 else (N - 1, N - 2, N - 3)
            g1 = [link[s] * from_x(s, f * N, N) + ends(edge[0][0][c][x0:x0 + 1, :], edge[1][0][c][x0:x0 + 1, :])
                  for c, f in enumerate(both)]
            ab0, ab1 = ab_plane(k, x0), ab_plane(k, x1)
            w0 = times(ab0, *g1)
            own = [trace(u_ref[f, base(x0):base(x0) + N, :], u_ref[f, base(x1):base(x1) + N, :]) for f in both]
            back = times(near_x[s][k], *own)
            corners = []
            for e in range(2):
                layers = []
                for layer in range(2):
                    relay = [from_t(e, 24 + s * 24 + f * 2 + layer, 1) for f in both]
                    layers.append(times(corner[s][e][k][layer], *relay))
                corners.append([trace(layers[0][c], layers[1][c]) for c in range(2)])
            rhs0, rhs1 = [], []
            for c, f in enumerate(both):
                ghost = link[s] * (from_x(s, FACE + f * N, N) + KEEP * back[c] + ends(corners[0][c], corners[1][c]))
                m1 = ends(edge[0][1][c][x1:x1 + 1, :], edge[1][1][c][x1:x1 + 1, :])
                m2 = ends(edge[0][1][c][x2:x2 + 1, :], edge[1][1][c][x2:x2 + 1, :])
                side0 = ends(ghost_y[0][c][x0:x0 + 1, :], ghost_y[1][c][x0:x0 + 1, :])
                side1 = ends(ghost_y[0][c][x1:x1 + 1, :], ghost_y[1][c][x1:x1 + 1, :])
                rhs0.append(row_neighbours(w0[c]) + lane_neighbours(w0[c]) + m1 + ghost + side0)
                rhs1.append(w0[c] + m2 + row_neighbours(m1) + lane_neighbours(m1) + side1)
            fix0, fix1 = times(ab0, *rhs0), times(ab1, *rhs1)
            at0, at1 = (0, 1) if s == 0 else (3, 2)
            for c, f in enumerate(both):
                planes_ref[f, at0 * N:(at0 + 1) * N, :] = w_ref[f, x0 * N:(x0 + 1) * N, :] + fix0[c]
                planes_ref[f, at1 * N:(at1 + 1) * N, :] = w_ref[f, x1 * N:(x1 + 1) * N, :] + fix1[c]
        for e in range(2):
            outer, inner = (0, 1) if e == 0 else (N - 1, N - 2)
            w0 = edge[e][1]
            rhs = [row_neighbours(w0[c]) + lane_neighbours(w0[c]) + ghost_y[e][c] for c in range(2)]
            fix0 = times(row_factors[k][e][0], *rhs)
            fix1 = times(row_factors[k][e][1], *w0)
            at0, at1 = (0, 1) if e == 0 else (3, 2)
            for c, f in enumerate(both):
                rows_ref[f, at0 * N:(at0 + 1) * N, :] = w_ref[f, pl.ds(outer, N, stride=N), :] + fix0[c]
                rows_ref[f, at1 * N:(at1 + 1) * N, :] = w_ref[f, pl.ds(inner, N, stride=N), :] + fix1[c]
    keep_ref[8 * N:, :] = keep_in_ref[...]
    send_ref[8 * N:, :] = send_in_ref[...]
    for ref, at in ((planes_ref, 0), (rows_ref, 4 * N)):
        term = [None, None]
        for comp in range(3):
            product = ref[6 + comp] * ref[3 + comp] + ref[9 + comp] * ref[comp]
            term[comp // 2] = product if comp % 2 == 0 else term[0] + product
        term_h, term_v = scale * term[0], scale * term[1]
        keep_ref[at:at + 4 * N, :] = jnp.where(odd_core, term_v, term_h)
        send_ref[at:at + 4 * N, :] = jnp.where(odd_core, term_h, term_v)


def put_boundary(step, block_ref, index, planes, rows):
    for at, y in enumerate((0, 1, N - 2, N - 1)):
        block_ref[(*index, pl.ds(y, STEP, stride=N), slice(None))] = rows(at)

    @pl.when(step == 0)
    def _():
        block_ref[(*index, slice(0, 2 * N), slice(None))] = planes(0)

    @pl.when(step == N // STEP - 1)
    def _():
        block_ref[(*index, slice(BLOCK - 2 * N, BLOCK), slice(None))] = planes(2 * N)


def field_kernel(w_ref, planes_ref, rows_ref, out_ref):
    step = pl.program_id(0)
    out_ref[...] = w_ref[0:6, pl.ds(pl.multiple_of(step * BLOCK, BLOCK), BLOCK), :]
    for f in range(6):
        put_boundary(
            step, out_ref, (f,),
            lambda at, f=f: planes_ref[f, at:at + 2 * N, :],
            lambda at, f=f: rows_ref[f, pl.ds(pl.multiple_of(at * N + step * STEP, 8), STEP), :],
        )


def gradient_kernel(mine_ref, other_ref, mine_b_ref, other_b_ref, ab_ref, sh_ref, sv_ref, gh_ref, gv_ref, total_ref):
    step = pl.program_id(0)
    odd_core = lax.rem(lax.axis_index("freq"), 2) == 1
    block = pl.ds(pl.multiple_of(step * BLOCK, BLOCK), BLOCK)
    mask = (ab_ref[0, block, :] > 0.0).astype(f32)
    for k, (sigma_ref, out_ref) in enumerate(((sh_ref, gh_ref), (sv_ref, gv_ref))):
        first = odd_core if k == 1 else jnp.logical_not(odd_core)
        for j in range(STEP):
            inner = jnp.clip(step * STEP + j - 2, 0, PIECES[0] - 1)
            rows = pl.ds(inner * INNER, INNER)
            total_ref[j * N + 2:(j + 1) * N - 2, :] = jnp.where(first, mine_ref[rows, :], other_ref[rows, :])

        def boundary(rows):
            return jnp.where(first, mine_b_ref[rows, :], other_b_ref[rows, :])

        @pl.when(step == N // STEP - 1)
        def _():
            for p in range(PIECES[1]):
                at, rows = (STEP - 2 - PIECES[1] + p) * N + 2, 8 * N + p * INNER
                total_ref[at:at + INNER, :] = boundary(slice(rows, rows + INNER))

        put_boundary(
            step, total_ref, (),
            lambda at: boundary(slice(at, at + 2 * N)),
            lambda at: boundary(pl.ds(pl.multiple_of((4 + at) * N + step * STEP, 8), STEP)),
        )
        out_ref[...] = sigma_ref[block, :] * mask * total_ref[...]


def swap_pairs(axis, odd):
    pairs_of = []
    for i in range(SUBS):
        at = [i % SX, i // SX]
        at[axis] += 1 if at[axis] % 2 == odd else -1
        if 0 <= at[axis] < SX:
            pairs_of.append((i, at[1] * SX + at[0]))
    return pairs_of


def swap(value, axis, odd):
    return lax.ppermute(value, "sub", swap_pairs(axis, odd))


def swap_freq(value, flip):
    return lax.ppermute(value, "freq", [(i, i ^ flip) for i in range(4)])


def sds(*shape):
    return jax.ShapeDtypeStruct(shape, f32)


def on_device(source, adjoint_source, sigma_h, sigma_v, seafloor, links, freq_index):
    steps = N // STEP
    src = in_hbm(source.reshape(6, N, N, NZ))
    adj = in_hbm(adjoint_source.reshape(6, N, N, NZ))
    cond_h = sigma_h.reshape(CELLS, NZ)
    cond_v = sigma_v.reshape(CELLS, NZ)
    cond_h4 = in_hbm(sigma_h.reshape(N, N, NZ))
    cond_v4 = in_hbm(sigma_v.reshape(N, N, NZ))
    floor = in_hbm(seafloor.reshape(N, N))
    links = in_hbm(links)
    smem = whole(pltpu.SMEM)

    def block3(size):
        return pl.BlockSpec((size, BLOCK, NZ), lambda i: (0, jnp.minimum(i, steps - 1), 0))

    block2 = pl.BlockSpec((BLOCK, NZ), lambda i: (jnp.minimum(i, steps - 1), 0))

    flat_src, flat_adj = in_hbm(source.reshape(6, CELLS, NZ)), in_hbm(adjoint_source.reshape(6, CELLS, NZ))
    flat_h, flat_v = in_hbm(cond_h), in_hbm(cond_v)
    last = N // 4 - 1
    field_x = pl.BlockSpec((6, 4 * N, NZ), lambda i: (0, i * last, 0))
    sigma_x = pl.BlockSpec((4 * N, NZ), lambda i: (i * last, 0))
    field_y = pl.BlockSpec((6, N, 8, NZ), lambda i: (0, 0, i * (N // 8 - 1), 0))
    sigma_y = pl.BlockSpec((N, 8, NZ), lambda i: (0, i * (N // 8 - 1), 0))
    px0, px1, py0, py1 = pl.pallas_call(
        strip_kernel,
        grid=(2,),
        in_specs=[smem] + [whole()] * 2 + [field_x, field_x, sigma_x, sigma_x, field_y, field_y, sigma_y, sigma_y],
        out_specs=[whole()] * 4,
        out_shape=[sds(X_ROWS, NZ), sds(X_ROWS, NZ), sds(Y_ROWS, NZ), sds(Y_ROWS, NZ)],
        scratch_shapes=[pltpu.VMEM((X_ROWS, NZ), f32)] * 2 + [pltpu.VMEM((Y_ROWS, NZ), f32)] * 2,
        compiler_params=params(14),
        cost_estimate=cost(10**6, 12 * 2**20),
        name="strips",
    )(freq_index, links, floor, flat_src, flat_adj, flat_h, flat_v, src, adj, cond_h4, cond_v4)
    ry1 = swap(py1, 1, 1)
    ry0 = swap(py0, 1, 0)
    rx1 = swap(px1, 0, 1)
    rx0 = swap(px0, 0, 0)

    u, ab, w, *terms = pl.pallas_call(
        solve_kernel,
        in_specs=[smem] + [whole()] * 5,
        out_specs=[whole()] * (3 + 2 * len(PIECES)),
        out_shape=[
            pltpu.VMEM((NF, ROWS, NZ), f32), pltpu.VMEM((4, CELLS, NZ), f32), pltpu.VMEM((NF, CELLS, NZ), f32),
        ] + [sds(size * INNER, NZ) for size in PIECES] * 2,
        scratch_shapes=[pltpu.VMEM((NF, ROWS, NZ), f32)],
        compiler_params=params(24),
        cost_estimate=cost(60 * NF * CELLS * NZ, 40 * 2**20),
        name="solve",
    )(
        freq_index, floor, source.reshape(6, CELLS, NZ), adjoint_source.reshape(6, CELLS, NZ), cond_h, cond_v
    )

    ty0, ty1 = pl.pallas_call(
        edge_kernel,
        in_specs=[whole()] * 4,
        out_specs=[whole()] * 2,
        out_shape=[sds(T_ROWS, NZ)] * 2,
        scratch_shapes=[pltpu.VMEM((T_ROWS, NZ), f32)] * 2,
        compiler_params=params(4),
        cost_estimate=cost(1000, 1000),
        name="edges",
    )(links, ab, rx0, rx1)
    rt1 = swap(ty1, 1, 1)
    rt0 = swap(ty0, 1, 0)

    mine = terms[0] + swap_freq(terms[2], 1)
    partner = swap_freq(mine, 2)

    planes, rows, keep_b, send_b = pl.pallas_call(
        boundary_kernel,
        in_specs=[smem] + [whole()] * 14,
        out_specs=[whole()] * 4,
        out_shape=[pltpu.VMEM((NF, 4 * N, NZ), f32)] * 2 + [sds(8 * N + PIECES[1] * INNER, NZ)] * 2,
        compiler_params=params(8),
        cost_estimate=cost(1000, 1000),
        name="boundary",
    )(freq_index, links, u, ab, w, py0, py1, rx0, rx1, ry0, ry1, rt0, rt1, terms[1], terms[3])

    forward = pl.pallas_call(
        field_kernel,
        grid=(steps,),
        in_specs=[whole()] * 3,
        out_specs=block3(6),
        out_shape=sds(6, CELLS, NZ),
        compiler_params=params(6),
        cost_estimate=cost(1000, 1000),
        name="field",
    )(w, planes, rows)

    mine_b = keep_b + swap_freq(send_b, 1)
    partner_b, partner, forward = lax.optimization_barrier((swap_freq(mine_b, 2), partner, forward))
    mine = mine + partner
    mine_b = mine_b + partner_b
    other = swap_freq(mine, 1)
    other_b = swap_freq(mine_b, 1)

    grad_h, grad_v = pl.pallas_call(
        gradient_kernel,
        grid=(steps,),
        in_specs=[whole()] * 7,
        out_specs=[block2, block2],
        out_shape=[sds(CELLS, NZ)] * 2,
        scratch_shapes=[pltpu.VMEM((BLOCK, NZ), f32)],
        compiler_params=params(6),
        cost_estimate=cost(1000, 1000),
        name="gradient",
    )(mine, other, mine_b, other_b, ab, cond_h, cond_v)

    return (
        forward.reshape(1, 1, 2, 3, N, N, NZ),
        grad_h.reshape(1, N, N, NZ),
        grad_v.reshape(1, N, N, NZ),
    )


def solution(mesh):
    return jax.shard_map(
        on_device,
        mesh=mesh,
        in_specs=(
            P("sub", None, None, None, None, None),
            P("freq", "sub", None, None, None, None, None),
            P("sub", None, None, None),
            P("sub", None, None, None),
            P("sub", None, None),
            P("sub", None),
            P("freq"),
        ),
        out_specs=(
            P("freq", "sub", None, None, None, None, None),
            P("sub", None, None, None),
            P("sub", None, None, None),
        ),
        check_vma=False,
    )
```

```python
import jax
import jax.numpy as jnp
from jax import lax
from jax.experimental import pallas as pl
from jax.experimental.pallas import tpu as pltpu
from jax.sharding import PartitionSpec as P

SX = 8
SUBS = 64
N = 32
NZ = 128
PIECES = (25, 3)
INNER = N - 4
PLANE = 40
ROWS = 34 * PLANE
STEP = 8
LAST = 16
BLOCK = STEP * N
CELLS = N * N
NF = 12
FACE = NF * N
X_S, X_R, X_C, X_ROWS = 2 * FACE, 2 * FACE + 64, 2 * FACE + 112, 2 * FACE + 120
Y_ROWS = 2 * FACE + 64
T_ROWS = 72

P_ROBIN = 0.25
OMEGA0 = 0.5
KEEP = 1.0 + P_ROBIN
f32 = jnp.float32


def whole(space=pltpu.VMEM):
    return pl.BlockSpec(memory_space=space)


def params(mib):
    return pltpu.CompilerParams(vmem_limit_bytes=mib * 2**20)


def in_hbm(value):
    return pltpu.with_memory_space_constraint(value, pltpu.HBM)


def cost(flops, size):
    return pl.CostEstimate(flops=flops, bytes_accessed=size, transcendentals=0)


def base(x):
    return (x + 1) * PLANE


def scale_of(freq_ref):
    return OMEGA0 * jnp.left_shift(jnp.int32(1), freq_ref[0]).astype(f32)


def link_of(links_ref, k):
    return links_ref[0:1, k:k + 1].astype(f32)


def lane_neighbours(u):
    lane = lax.broadcasted_iota(jnp.int32, u.shape, 1)
    before = jnp.where(lane == 0, 0.0, pltpu.roll(u, 1, 1))
    after = jnp.where(lane == NZ - 1, 0.0, pltpu.roll(u, NZ - 1, 1))
    return before + after


def row_neighbours(u):
    row = lax.broadcasted_iota(jnp.int32, u.shape, 0)
    before = jnp.where(row == 0, 0.0, pltpu.roll(u, 1, 0))
    after = jnp.where(row == N - 1, 0.0, pltpu.roll(u, N - 1, 0))
    return before + after


def factors(shift):
    inverse = 1.0 / (36.0 + shift * shift)
    return jnp.where(shift > 0.0, 6.0 * inverse, 0.0), shift * inverse


def times(ab, re, im):
    a, b = ab
    return a * re + b * im, a * im - b * re


def pairs():
    for solve in range(2):
        for comp in range(3):
            yield solve * 6 + comp, solve * 6 + 3 + comp, comp // 2


def trace(outer, inner):
    return KEEP * outer - P_ROBIN * inner


def stencil(ref, f, x):
    start = base(x)
    centre = ref[f, pl.ds(start, N), :]
    total = ref[f, pl.ds(start - PLANE, N), :] + ref[f, pl.ds(start + PLANE, N), :]
    total = total + (ref[f, pl.ds(start - 1, N), :] + ref[f, pl.ds(start + 1, N), :])
    return total + lane_neighbours(centre)


def floor_column(floor_ref, x, first, size):
    floor = floor_ref[pl.ds(x, 1), :].astype(f32)
    row = lax.broadcasted_iota(jnp.int32, (size, N), 0) + first
    col = lax.broadcasted_iota(jnp.int32, (size, N), 1)
    return jnp.sum(jnp.where(row == col, floor, 0.0), axis=1, keepdims=True)


def mask_of(column):
    depth = lax.broadcasted_iota(jnp.int32, (column.shape[0], NZ), 1).astype(f32)
    return (depth >= column).astype(f32)


def parity():
    sub = lax.axis_index("sub")
    return lax.rem(sub, 2) == 1, lax.rem(lax.div(sub, SX), 2) == 1


def face(out_ref, shift, field, keep=None):
    ab = [[factors(value) for value in layer] for layer in shift]
    for k in range(2):
        out_ref[X_S + k * N:X_S + (k + 1) * N, :] = shift[0][k]
    for fr, fi, k in pairs():
        u = [times(ab[l][k], field(fr, l), field(fi, l)) for l in range(3)]
        v = []
        for l in range(2):
            near = [u[l + 1][c] if l == 0 else u[0][c] + u[2][c] for c in range(2)]
            total = [near[c] + row_neighbours(u[l][c]) + lane_neighbours(u[l][c]) for c in range(2)]
            new = times(ab[l][k], *total)
            v.append([u[l][c] + new[c] for c in range(2)])
        for c, f in enumerate((fr, fi)):
            out_ref[f * N:(f + 1) * N, :] = trace(u[0][c], u[1][c])
            out_ref[FACE + f * N:FACE + (f + 1) * N, :] = trace(v[0][c], v[1][c])
            if keep is not None:
                keep(f, u[0][c], u[1][c])


def strip_kernel(
    freq_ref, links_ref, floor_ref,
    srcx_ref, adjx_ref, shx_ref, svx_ref, srcy_ref, adjy_ref, shy_ref, svy_ref,
    px0_ref, px1_ref, py0_ref, py1_ref, xl_ref, xh_ref, yl_ref, yh_ref,
):
    step = pl.program_id(0)
    scale = scale_of(freq_ref)
    odd_x, odd_y = parity()
    fields = [ref.reshape(6, N * 8, NZ) for ref in (srcy_ref, adjy_ref)]
    sigmas = [ref.reshape(N * 8, NZ) for ref in (shy_ref, svy_ref)]

    def side(s, x_ref, y_ref):
        def plane(l):
            return slice((3 - l) * N, (4 - l) * N) if s else slice(l * N, (l + 1) * N)

        def line(l):
            return pl.ds(7 - l if s else l, N, stride=8)

        def field_x(f, l):
            return srcx_ref[f, plane(l), :] if f < 6 else adjx_ref[f - 6, plane(l), :]

        def field_y(f, l):
            return fields[f // 6][f % 6, line(l), :]

        def relay(f, outer, inner):
            for e in range(2):
                for l, value in enumerate((outer, inner)):
                    at = X_R + e * 24 + f * 2 + l
                    row = [value[y:y + 1, :] for y in ((N - 1, N - 2) if e else (0, 1))]
                    x_ref[at:at + 1, :] = link_of(links_ref, 2 + e) * trace(*row)

        layers = [N - 1 - l if s else l for l in range(3)]
        masks = [mask_of(floor_column(floor_ref, x, 0, N)) for x in layers]
        shift = [[scale * ref[plane(l), :] * masks[l] for ref in (shx_ref, svx_ref)] for l in range(3)]
        face(x_ref, shift, field_x, relay)
        for end in range(2):
            for k in range(2):
                for l in range(2):
                    at = X_C + end * 4 + k * 2 + l
                    x_ref[at:at + 1, :] = shift[l][k][end * (N - 1):end * (N - 1) + 1, :]
        masks = [mask_of(floor_ref[:, y:y + 1].astype(f32)) for y in layers]
        shift = [[scale * ref[line(l), :] * masks[l] for ref in sigmas] for l in range(3)]
        face(y_ref, shift, field_y)

    @pl.when(step == 0)
    def _():
        side(0, xl_ref, yl_ref)

    @pl.when(step == 1)
    def _():
        side(1, xh_ref, yh_ref)
        low, high = xl_ref[...], xh_ref[...]
        px0_ref[...] = jnp.where(odd_x, low, high)
        px1_ref[...] = jnp.where(odd_x, high, low)
        low, high = yl_ref[...], yh_ref[...]
        py0_ref[...] = jnp.where(odd_y, low, high)
        py1_ref[...] = jnp.where(odd_y, high, low)


def edge_kernel(links_ref, ab_ref, rx0_ref, rx1_ref, ty0_ref, ty1_ref, tl_ref, th_ref):
    odd_x, odd_y = parity()

    def from_x(side, rows):
        first, second = rx0_ref[rows, :], rx1_ref[rows, :]
        return jnp.where(odd_x, first, second) if side == 0 else jnp.where(odd_x, second, first)

    for e, t_ref in enumerate((tl_ref, th_ref)):
        outer, inner = (0, 1) if e == 0 else (N - 1, N - 2)
        for side in range(2):
            link = link_of(links_ref, side)
            x = side * (N - 1)
            for fr, fi, k in pairs():
                layers = []
                for y in (outer, inner):
                    at = x * N + y
                    ab = (ab_ref[2 * k, at:at + 1, :], ab_ref[2 * k + 1, at:at + 1, :])
                    re = link * from_x(side, slice(fr * N + y, fr * N + y + 1))
                    im = link * from_x(side, slice(fi * N + y, fi * N + y + 1))
                    layers.append(times(ab, re, im))
                t_ref[side * NF + fr:side * NF + fr + 1, :] = trace(layers[0][0], layers[1][0])
                t_ref[side * NF + fi:side * NF + fi + 1, :] = trace(layers[0][1], layers[1][1])
            at = X_R + e * 24
            t_ref[24 + side * 24:48 + side * 24, :] = from_x(side, slice(at, at + 24))
    low, high = tl_ref[...], th_ref[...]
    ty0_ref[...] = jnp.where(odd_y, low, high)
    ty1_ref[...] = jnp.where(odd_y, high, low)


def solve_kernel(
    freq_ref, floor_ref, src_ref, adj_ref, sh_ref, sv_ref,
    u_ref, ab_ref, w_ref, *refs,
):
    scale = scale_of(freq_ref)
    odd_core = lax.rem(lax.axis_index("freq"), 2) == 1
    count = len(PIECES)
    keep_refs, send_refs, v_ref = refs[:count], refs[count:2 * count], refs[2 * count]
    zeros = jnp.zeros((PLANE, NZ), f32)
    for f in range(NF):
        for ref in (u_ref, v_ref):
            ref[f, 0:PLANE, :] = zeros
            ref[f, ROWS - PLANE:ROWS, :] = zeros

    def first_update(x, carry):
        there = pl.ds(pl.multiple_of(x * N, N), N)
        start = pl.multiple_of(base(x), 8)
        mask = mask_of(floor_column(floor_ref, x, 0, N))
        ab = []
        for k, ref in enumerate((sh_ref, sv_ref)):
            ab.append(factors(scale * ref[there, :] * mask))
            ab_ref[2 * k, there, :] = ab[k][0]
            ab_ref[2 * k + 1, there, :] = ab[k][1]
        zeros = jnp.zeros((8, NZ), f32)
        for fr, fi, k in pairs():
            ref, g = (src_ref, 0) if fr < 6 else (adj_ref, 6)
            re, im = times(ab[k], ref[fr - g, there, :], ref[fi - g, there, :])
            for f, value in ((fr, re), (fi, im)):
                u_ref[f, pl.ds(start, N), :] = value
                u_ref[f, pl.ds(start + N, 8), :] = zeros
                v_ref[f, pl.ds(start + N, 8), :] = zeros
        return carry

    lax.fori_loop(0, N, first_update, 0, unroll=4)

    def second_update(x, carry):
        there = pl.ds(pl.multiple_of(x * N, N), N)
        start = pl.multiple_of(base(x), 8)
        ab = [(ab_ref[2 * k, there, :], ab_ref[2 * k + 1, there, :]) for k in range(2)]
        for fr, fi, k in pairs():
            re, im = times(ab[k], stencil(u_ref, fr, x), stencil(u_ref, fi, x))
            v_ref[fr, pl.ds(start, N), :] = u_ref[fr, pl.ds(start, N), :] + re
            v_ref[fi, pl.ds(start, N), :] = u_ref[fi, pl.ds(start, N), :] + im
        return carry

    lax.fori_loop(0, N, second_update, 0, unroll=4)

    def last_update(x):
        there = pl.ds(pl.multiple_of(x * N, N), N)
        start = pl.multiple_of(base(x), 8)
        ab = [(ab_ref[2 * k, there, :], ab_ref[2 * k + 1, there, :]) for k in range(2)]
        term = [None, None]
        for comp in range(3):
            k = comp // 2
            new = []
            for solve in range(2):
                fr, fi = solve * 6 + comp, solve * 6 + 3 + comp
                re, im = times(ab[k], stencil(v_ref, fr, x), stencil(v_ref, fi, x))
                re = re + u_ref[fr, pl.ds(start, N), :]
                im = im + u_ref[fi, pl.ds(start, N), :]
                w_ref[fr, there, :] = re
                w_ref[fi, there, :] = im
                new.append((re, im))
            product = new[1][0] * new[0][1] + new[1][1] * new[0][0]
            term[k] = product if term[k] is None else term[k] + product
        return term

    for x in (0, 1, N - 2, N - 1):
        last_update(x)
    first = 2
    for size, keep_ref, send_ref in zip(PIECES, keep_refs, send_refs):
        def plane(j, carry, first=first, keep_ref=keep_ref, send_ref=send_ref):
            here = pl.ds(j * INNER, INNER)
            term = last_update(first + j)
            term_h, term_v = scale * term[0], scale * term[1]
            keep_ref[here, :] = jnp.where(odd_core, term_v, term_h)[2:N - 2, :]
            send_ref[here, :] = jnp.where(odd_core, term_h, term_v)[2:N - 2, :]
            return carry

        lax.fori_loop(0, size, plane, 0, unroll=4)
        first += size


def gather_kernel(ab_ref, w_ref, abr_ref, wr_ref):
    for at, y in enumerate((0, 1, N - 2, N - 1)):
        out = slice(at * N, (at + 1) * N)
        for k in range(4):
            abr_ref[k, out, :] = ab_ref[k, pl.ds(y, N, stride=N), :]
        for f in range(NF):
            wr_ref[f, out, :] = w_ref[f, pl.ds(y, N, stride=N), :]


def boundary_kernel(
    freq_ref, links_ref, u_ref, ab_ref, w_ref, abr_ref, wr_ref, py0_ref, py1_ref,
    rx0_ref, rx1_ref, ry0_ref, ry1_ref, rt0_ref, rt1_ref, keep_in_ref, send_in_ref,
    planes_ref, rows_ref, keep_ref, send_ref,
):
    scale = scale_of(freq_ref)
    odd_x, odd_y = parity()
    odd_core = lax.rem(lax.axis_index("freq"), 2) == 1
    link = [link_of(links_ref, k) for k in range(4)]
    row = lax.broadcasted_iota(jnp.int32, (N, NZ), 0)

    def pick(odd, side, first_ref, second_ref, rows):
        first, second = first_ref[rows, :], second_ref[rows, :]
        return jnp.where(odd, first, second) if side == 0 else jnp.where(odd, second, first)

    def from_x(side, at, size):
        return pick(odd_x, side, rx0_ref, rx1_ref, slice(at, at + size))

    def from_y(side, at, size):
        return pick(odd_y, side, ry0_ref, ry1_ref, slice(at, at + size))

    def from_t(side, at, size):
        return pick(odd_y, side, rt0_ref, rt1_ref, slice(at, at + size))

    def ends(first, last):
        return jnp.where(row == 0, first, jnp.where(row == N - 1, last, 0.0))

    def ab_plane(k, x):
        return ab_ref[2 * k, x * N:(x + 1) * N, :], ab_ref[2 * k + 1, x * N:(x + 1) * N, :]

    def ab_row(k, at):
        return abr_ref[2 * k, at * N:(at + 1) * N, :], abr_ref[2 * k + 1, at * N:(at + 1) * N, :]

    near_x = [[factors(from_x(s, X_S + k * N, N)) for k in range(2)] for s in range(2)]
    near_y = [[factors(from_y(s, X_S + k * N, N)) for k in range(2)] for s in range(2)]
    corner = [[[[factors(from_x(s, X_C + e * 4 + k * 2 + layer, 1)) for layer in range(2)]
                for k in range(2)] for e in range(2)] for s in range(2)]

    row_factors = [[[ab_row(k, at) for at in ats] for ats in ((0, 1), (3, 2))] for k in range(2)]

    for fr, fi, k in pairs():
        both = (fr, fi)
        edge, ghost_y = [], []
        for e in range(2):
            g1 = [link[2 + e] * from_y(e, f * N, N) for f in both]
            edge.append((g1, times(row_factors[k][e][0], *g1)))
            own = [pick(odd_y, e, py0_ref, py1_ref, slice(f * N, (f + 1) * N)) for f in both]
            back = times(near_y[e][k], *own)
            ghost_y.append([
                link[2 + e] * (from_y(e, FACE + f * N, N) + KEEP * back[c] + ends(from_t(e, f, 1), from_t(e, NF + f, 1)))
                for c, f in enumerate(both)
            ])
        for s in range(2):
            x0, x1, x2 = (0, 1, 2) if s == 0 else (N - 1, N - 2, N - 3)
            g1 = [link[s] * from_x(s, f * N, N) + ends(edge[0][0][c][x0:x0 + 1, :], edge[1][0][c][x0:x0 + 1, :])
                  for c, f in enumerate(both)]
            ab0, ab1 = ab_plane(k, x0), ab_plane(k, x1)
            w0 = times(ab0, *g1)
            own = [trace(u_ref[f, base(x0):base(x0) + N, :], u_ref[f, base(x1):base(x1) + N, :]) for f in both]
            back = times(near_x[s][k], *own)
            corners = []
            for e in range(2):
                layers = []
                for layer in range(2):
                    relay = [from_t(e, 24 + s * 24 + f * 2 + layer, 1) for f in both]
                    layers.append(times(corner[s][e][k][layer], *relay))
                corners.append([trace(layers[0][c], layers[1][c]) for c in range(2)])
            rhs0, rhs1 = [], []
            for c, f in enumerate(both):
                ghost = link[s] * (from_x(s, FACE + f * N, N) + KEEP * back[c] + ends(corners[0][c], corners[1][c]))
                m1 = ends(edge[0][1][c][x1:x1 + 1, :], edge[1][1][c][x1:x1 + 1, :])
                m2 = ends(edge[0][1][c][x2:x2 + 1, :], edge[1][1][c][x2:x2 + 1, :])
                side0 = ends(ghost_y[0][c][x0:x0 + 1, :], ghost_y[1][c][x0:x0 + 1, :])
                side1 = ends(ghost_y[0][c][x1:x1 + 1, :], ghost_y[1][c][x1:x1 + 1, :])
                rhs0.append(row_neighbours(w0[c]) + lane_neighbours(w0[c]) + m1 + ghost + side0)
                rhs1.append(w0[c] + m2 + row_neighbours(m1) + lane_neighbours(m1) + side1)
            fix0, fix1 = times(ab0, *rhs0), times(ab1, *rhs1)
            at0, at1 = (0, 1) if s == 0 else (3, 2)
            for c, f in enumerate(both):
                planes_ref[f, at0 * N:(at0 + 1) * N, :] = w_ref[f, x0 * N:(x0 + 1) * N, :] + fix0[c]
                planes_ref[f, at1 * N:(at1 + 1) * N, :] = w_ref[f, x1 * N:(x1 + 1) * N, :] + fix1[c]
        for e in range(2):
            w0 = edge[e][1]
            rhs = [row_neighbours(w0[c]) + lane_neighbours(w0[c]) + ghost_y[e][c] for c in range(2)]
            fix0 = times(row_factors[k][e][0], *rhs)
            fix1 = times(row_factors[k][e][1], *w0)
            at0, at1 = (0, 1) if e == 0 else (3, 2)
            for c, f in enumerate(both):
                rows_ref[f, at0 * N:(at0 + 1) * N, :] = wr_ref[f, at0 * N:(at0 + 1) * N, :] + fix0[c]
                rows_ref[f, at1 * N:(at1 + 1) * N, :] = wr_ref[f, at1 * N:(at1 + 1) * N, :] + fix1[c]
    keep_ref[8 * N:, :] = keep_in_ref[...]
    send_ref[8 * N:, :] = send_in_ref[...]
    for ref, at in ((planes_ref, 0), (rows_ref, 4 * N)):
        term = [None, None]
        for comp in range(3):
            product = ref[6 + comp] * ref[3 + comp] + ref[9 + comp] * ref[comp]
            term[comp // 2] = product if comp % 2 == 0 else term[0] + product
        term_h, term_v = scale * term[0], scale * term[1]
        keep_ref[at:at + 4 * N, :] = jnp.where(odd_core, term_v, term_h)
        send_ref[at:at + 4 * N, :] = jnp.where(odd_core, term_h, term_v)


def put_boundary(step, block_ref, index, planes, rows, size=STEP):
    for at, y in enumerate((0, 1, N - 2, N - 1)):
        block_ref[(*index, pl.ds(y, size, stride=N), slice(None))] = rows(at)

    @pl.when(step == 0)
    def _():
        block_ref[(*index, slice(0, 2 * N), slice(None))] = planes(0)

    @pl.when(step == N // size - 1)
    def _():
        block_ref[(*index, slice((size - 2) * N, size * N), slice(None))] = planes(2 * N)


def field_kernel(w_ref, planes_ref, rows_ref, out_ref):
    step = pl.program_id(0)
    out_ref[...] = w_ref[0:6, pl.ds(pl.multiple_of(step * BLOCK, BLOCK), BLOCK), :]
    for f in range(6):
        put_boundary(
            step, out_ref, (f,),
            lambda at, f=f: planes_ref[f, at:at + 2 * N, :],
            lambda at, f=f: rows_ref[f, pl.ds(pl.multiple_of(at * N + step * STEP, 8), STEP), :],
        )


def gradient_kernel(mine_ref, other_ref, mine_b_ref, other_b_ref, ab_ref, sh_ref, sv_ref, gh_ref, gv_ref, total_ref):
    step = pl.program_id(0)
    odd_core = lax.rem(lax.axis_index("freq"), 2) == 1
    block = pl.ds(pl.multiple_of(step * LAST * N, LAST * N), LAST * N)
    mask = (ab_ref[0, block, :] > 0.0).astype(f32)
    for k, (sigma_ref, out_ref) in enumerate(((sh_ref, gh_ref), (sv_ref, gv_ref))):
        first = odd_core if k == 1 else jnp.logical_not(odd_core)
        for j in range(LAST):
            inner = jnp.clip(step * LAST + j - 2, 0, PIECES[0] - 1)
            rows = pl.ds(inner * INNER, INNER)
            total_ref[j * N + 2:(j + 1) * N - 2, :] = jnp.where(first, mine_ref[rows, :], other_ref[rows, :])

        def boundary(rows):
            return jnp.where(first, mine_b_ref[rows, :], other_b_ref[rows, :])

        @pl.when(step == N // LAST - 1)
        def _():
            for p in range(PIECES[1]):
                at, rows = (LAST - 2 - PIECES[1] + p) * N + 2, 8 * N + p * INNER
                total_ref[at:at + INNER, :] = boundary(slice(rows, rows + INNER))

        put_boundary(
            step, total_ref, (),
            lambda at: boundary(slice(at, at + 2 * N)),
            lambda at: boundary(pl.ds(pl.multiple_of((4 + at) * N + step * LAST, 8), LAST)),
            LAST,
        )
        out_ref[...] = sigma_ref[block, :] * mask * total_ref[...]


def swap_pairs(axis, odd):
    pairs_of = []
    for i in range(SUBS):
        at = [i % SX, i // SX]
        at[axis] += 1 if at[axis] % 2 == odd else -1
        if 0 <= at[axis] < SX:
            pairs_of.append((i, at[1] * SX + at[0]))
    return pairs_of


def swap(value, axis, odd):
    return lax.ppermute(value, "sub", swap_pairs(axis, odd))


def swap_freq(value, flip):
    return lax.ppermute(value, "freq", [(i, i ^ flip) for i in range(4)])


def sds(*shape):
    return jax.ShapeDtypeStruct(shape, f32)


def on_device(source, adjoint_source, sigma_h, sigma_v, seafloor, links, freq_index):
    steps = N // STEP
    src = in_hbm(source.reshape(6, N, N, NZ))
    adj = in_hbm(adjoint_source.reshape(6, N, N, NZ))
    cond_h = sigma_h.reshape(CELLS, NZ)
    cond_v = sigma_v.reshape(CELLS, NZ)
    cond_h4 = in_hbm(sigma_h.reshape(N, N, NZ))
    cond_v4 = in_hbm(sigma_v.reshape(N, N, NZ))
    floor = in_hbm(seafloor.reshape(N, N))
    links = in_hbm(links)
    smem = whole(pltpu.SMEM)

    def block3(size):
        return pl.BlockSpec((size, BLOCK, NZ), lambda i: (0, jnp.minimum(i, steps - 1), 0))

    block2 = pl.BlockSpec((BLOCK, NZ), lambda i: (jnp.minimum(i, steps - 1), 0))

    flat_src, flat_adj = in_hbm(source.reshape(6, CELLS, NZ)), in_hbm(adjoint_source.reshape(6, CELLS, NZ))
    flat_h, flat_v = in_hbm(cond_h), in_hbm(cond_v)
    last = N // 4 - 1
    field_x = pl.BlockSpec((6, 4 * N, NZ), lambda i: (0, i * last, 0))
    sigma_x = pl.BlockSpec((4 * N, NZ), lambda i: (i * last, 0))
    field_y = pl.BlockSpec((6, N, 8, NZ), lambda i: (0, 0, i * (N // 8 - 1), 0))
    sigma_y = pl.BlockSpec((N, 8, NZ), lambda i: (0, i * (N // 8 - 1), 0))
    px0, px1, py0, py1 = pl.pallas_call(
        strip_kernel,
        grid=(2,),
        in_specs=[smem] + [whole()] * 2 + [field_x, field_x, sigma_x, sigma_x, field_y, field_y, sigma_y, sigma_y],
        out_specs=[whole()] * 4,
        out_shape=[sds(X_ROWS, NZ), sds(X_ROWS, NZ), sds(Y_ROWS, NZ), sds(Y_ROWS, NZ)],
        scratch_shapes=[pltpu.VMEM((X_ROWS, NZ), f32)] * 2 + [pltpu.VMEM((Y_ROWS, NZ), f32)] * 2,
        compiler_params=params(14),
        cost_estimate=cost(10**6, 12 * 2**20),
        name="strips",
    )(freq_index, links, floor, flat_src, flat_adj, flat_h, flat_v, src, adj, cond_h4, cond_v4)
    ry1 = swap(py1, 1, 1)
    ry0 = swap(py0, 1, 0)
    rx1 = swap(px1, 0, 1)
    rx0 = swap(px0, 0, 0)

    u, ab, w, *terms = pl.pallas_call(
        solve_kernel,
        in_specs=[smem] + [whole()] * 5,
        out_specs=[whole()] * (3 + 2 * len(PIECES)),
        out_shape=[
            pltpu.VMEM((NF, ROWS, NZ), f32), pltpu.VMEM((4, CELLS, NZ), f32), pltpu.VMEM((NF, CELLS, NZ), f32),
        ] + [sds(size * INNER, NZ) for size in PIECES] * 2,
        scratch_shapes=[pltpu.VMEM((NF, ROWS, NZ), f32)],
        compiler_params=params(24),
        cost_estimate=cost(60 * NF * CELLS * NZ, 40 * 2**20),
        name="solve",
    )(
        freq_index, floor, source.reshape(6, CELLS, NZ), adjoint_source.reshape(6, CELLS, NZ), cond_h, cond_v
    )

    ty0, ty1 = pl.pallas_call(
        edge_kernel,
        in_specs=[whole()] * 4,
        out_specs=[whole()] * 2,
        out_shape=[sds(T_ROWS, NZ)] * 2,
        scratch_shapes=[pltpu.VMEM((T_ROWS, NZ), f32)] * 2,
        compiler_params=params(4),
        cost_estimate=cost(1000, 1000),
        name="edges",
    )(links, ab, rx0, rx1)
    rt1 = swap(ty1, 1, 1)
    rt0 = swap(ty0, 1, 0)

    mine = terms[0] + swap_freq(terms[2], 1)
    partner = swap_freq(mine, 2)

    abr, wr = pl.pallas_call(
        gather_kernel,
        in_specs=[whole()] * 2,
        out_specs=[whole()] * 2,
        out_shape=[pltpu.VMEM((4, 4 * N, NZ), f32), pltpu.VMEM((NF, 4 * N, NZ), f32)],
        compiler_params=params(4),
        cost_estimate=cost(1000, 1000),
        name="gather",
    )(ab, w)
    planes, rows, keep_b, send_b = pl.pallas_call(
        boundary_kernel,
        in_specs=[smem] + [whole()] * 16,
        out_specs=[whole()] * 4,
        out_shape=[pltpu.VMEM((NF, 4 * N, NZ), f32)] * 2 + [sds(8 * N + PIECES[1] * INNER, NZ)] * 2,
        compiler_params=params(8),
        cost_estimate=cost(1000, 1000),
        name="boundary",
    )(freq_index, links, u, ab, w, abr, wr, py0, py1, rx0, rx1, ry0, ry1, rt0, rt1, terms[1], terms[3])

    forward = pl.pallas_call(
        field_kernel,
        grid=(steps,),
        in_specs=[whole()] * 3,
        out_specs=block3(6),
        out_shape=sds(6, CELLS, NZ),
        compiler_params=params(6),
        cost_estimate=cost(1000, 1000),
        name="field",
    )(w, planes, rows)

    mine_b = keep_b + swap_freq(send_b, 1)
    partner_b, partner, forward = lax.optimization_barrier((swap_freq(mine_b, 2), partner, forward))
    mine = mine + partner
    mine_b = mine_b + partner_b
    other = swap_freq(mine, 1)
    other_b = swap_freq(mine_b, 1)

    grad_h, grad_v = pl.pallas_call(
        gradient_kernel,
        grid=(N // LAST,),
        in_specs=[whole()] * 7,
        out_specs=[pl.BlockSpec((LAST * N, NZ), lambda i: (i, 0))] * 2,
        out_shape=[sds(CELLS, NZ)] * 2,
        scratch_shapes=[pltpu.VMEM((LAST * N, NZ), f32)],
        compiler_params=params(6),
        cost_estimate=cost(1000, 1000),
        name="gradient",
    )(mine, other, mine_b, other_b, ab, cond_h, cond_v)

    return (
        forward.reshape(1, 1, 2, 3, N, N, NZ),
        grad_h.reshape(1, N, N, NZ),
        grad_v.reshape(1, N, N, NZ),
    )


def solution(mesh):
    return jax.shard_map(
        on_device,
        mesh=mesh,
        in_specs=(
            P("sub", None, None, None, None, None),
            P("freq", "sub", None, None, None, None, None),
            P("sub", None, None, None),
            P("sub", None, None, None),
            P("sub", None, None),
            P("sub", None),
            P("freq"),
        ),
        out_specs=(
            P("freq", "sub", None, None, None, None, None),
            P("sub", None, None, None),
            P("sub", None, None, None),
        ),
        check_vma=False,
    )
```

```python
import jax
import jax.numpy as jnp
from jax import lax
from jax.experimental import pallas as pl
from jax.experimental.pallas import tpu as pltpu
from jax.sharding import PartitionSpec as P

SX = 8
SUBS = 64
N = 32
NZ = 128
PIECES = (25, 3)
PIECE_ROWS = (25 * 28 + 4, 3 * 28 + 4)
INNER = N - 4
PLANE = 40
ROWS = 34 * PLANE
STEP = 8
LAST = 16
BLOCK = STEP * N
CELLS = N * N
NF = 12
FACE = NF * N
X_S, X_R, X_C, X_ROWS = 2 * FACE, 2 * FACE + 64, 2 * FACE + 112, 2 * FACE + 120
Y_ROWS = 2 * FACE + 64
T_ROWS = 72

P_ROBIN = 0.25
OMEGA0 = 0.5
KEEP = 1.0 + P_ROBIN
f32 = jnp.float32


def whole(space=pltpu.VMEM):
    return pl.BlockSpec(memory_space=space)


def params(mib):
    return pltpu.CompilerParams(vmem_limit_bytes=mib * 2**20)


def in_hbm(value):
    return pltpu.with_memory_space_constraint(value, pltpu.HBM)


def cost(flops, size):
    return pl.CostEstimate(flops=flops, bytes_accessed=size, transcendentals=0)


def base(x):
    return (x + 1) * PLANE


def scale_of(freq_ref):
    return OMEGA0 * jnp.left_shift(jnp.int32(1), freq_ref[0]).astype(f32)


def link_of(links_ref, k):
    return links_ref[0:1, k:k + 1].astype(f32)


def lane_neighbours(u):
    lane = lax.broadcasted_iota(jnp.int32, u.shape, 1)
    before = jnp.where(lane == 0, 0.0, pltpu.roll(u, 1, 1))
    after = jnp.where(lane == NZ - 1, 0.0, pltpu.roll(u, NZ - 1, 1))
    return before + after


def row_neighbours(u):
    row = lax.broadcasted_iota(jnp.int32, u.shape, 0)
    before = jnp.where(row == 0, 0.0, pltpu.roll(u, 1, 0))
    after = jnp.where(row == N - 1, 0.0, pltpu.roll(u, N - 1, 0))
    return before + after


def factors(shift):
    inverse = 1.0 / (36.0 + shift * shift)
    return jnp.where(shift > 0.0, 6.0 * inverse, 0.0), shift * inverse


def times(ab, re, im):
    a, b = ab
    return a * re + b * im, a * im - b * re


def pairs():
    for solve in range(2):
        for comp in range(3):
            yield solve * 6 + comp, solve * 6 + 3 + comp, comp // 2


def trace(outer, inner):
    return KEEP * outer - P_ROBIN * inner


def stencil(ref, f, x):
    start = base(x)
    centre = ref[f, pl.ds(start, N), :]
    total = ref[f, pl.ds(start - PLANE, N), :] + ref[f, pl.ds(start + PLANE, N), :]
    total = total + (ref[f, pl.ds(start - 1, N), :] + ref[f, pl.ds(start + 1, N), :])
    return total + lane_neighbours(centre)


def floor_column(floor_ref, x, first, size):
    floor = floor_ref[pl.ds(x, 1), :].astype(f32)
    row = lax.broadcasted_iota(jnp.int32, (size, N), 0) + first
    col = lax.broadcasted_iota(jnp.int32, (size, N), 1)
    return jnp.sum(jnp.where(row == col, floor, 0.0), axis=1, keepdims=True)


def mask_of(column):
    depth = lax.broadcasted_iota(jnp.int32, (column.shape[0], NZ), 1).astype(f32)
    return (depth >= column).astype(f32)


def parity():
    sub = lax.axis_index("sub")
    return lax.rem(sub, 2) == 1, lax.rem(lax.div(sub, SX), 2) == 1


def face(out_ref, shift, field, keep=None):
    ab = [[factors(value) for value in layer] for layer in shift]
    for k in range(2):
        out_ref[X_S + k * N:X_S + (k + 1) * N, :] = shift[0][k]
    for fr, fi, k in pairs():
        u = [times(ab[l][k], field(fr, l), field(fi, l)) for l in range(3)]
        v = []
        for l in range(2):
            near = [u[l + 1][c] if l == 0 else u[0][c] + u[2][c] for c in range(2)]
            total = [near[c] + row_neighbours(u[l][c]) + lane_neighbours(u[l][c]) for c in range(2)]
            new = times(ab[l][k], *total)
            v.append([u[l][c] + new[c] for c in range(2)])
        for c, f in enumerate((fr, fi)):
            out_ref[f * N:(f + 1) * N, :] = trace(u[0][c], u[1][c])
            out_ref[FACE + f * N:FACE + (f + 1) * N, :] = trace(v[0][c], v[1][c])
            if keep is not None:
                keep(f, u[0][c], u[1][c])


def strip_kernel(
    freq_ref, links_ref, floor_ref,
    srcx_ref, adjx_ref, shx_ref, svx_ref, srcy_ref, adjy_ref, shy_ref, svy_ref,
    px0_ref, px1_ref, py0_ref, py1_ref, xl_ref, xh_ref, yl_ref, yh_ref,
):
    step = pl.program_id(0)
    scale = scale_of(freq_ref)
    odd_x, odd_y = parity()
    fields = [ref.reshape(6, N * 8, NZ) for ref in (srcy_ref, adjy_ref)]
    sigmas = [ref.reshape(N * 8, NZ) for ref in (shy_ref, svy_ref)]

    def side(s, x_ref, y_ref):
        def plane(l):
            return slice((3 - l) * N, (4 - l) * N) if s else slice(l * N, (l + 1) * N)

        def line(l):
            return pl.ds(7 - l if s else l, N, stride=8)

        def field_x(f, l):
            return srcx_ref[f, plane(l), :] if f < 6 else adjx_ref[f - 6, plane(l), :]

        def field_y(f, l):
            return fields[f // 6][f % 6, line(l), :]

        def relay(f, outer, inner):
            for e in range(2):
                for l, value in enumerate((outer, inner)):
                    at = X_R + e * 24 + f * 2 + l
                    row = [value[y:y + 1, :] for y in ((N - 1, N - 2) if e else (0, 1))]
                    x_ref[at:at + 1, :] = link_of(links_ref, 2 + e) * trace(*row)

        layers = [N - 1 - l if s else l for l in range(3)]
        masks = [mask_of(floor_column(floor_ref, x, 0, N)) for x in layers]
        shift = [[scale * ref[plane(l), :] * masks[l] for ref in (shx_ref, svx_ref)] for l in range(3)]
        face(x_ref, shift, field_x, relay)
        for end in range(2):
            for k in range(2):
                for l in range(2):
                    at = X_C + end * 4 + k * 2 + l
                    x_ref[at:at + 1, :] = shift[l][k][end * (N - 1):end * (N - 1) + 1, :]
        masks = [mask_of(floor_ref[:, y:y + 1].astype(f32)) for y in layers]
        shift = [[scale * ref[line(l), :] * masks[l] for ref in sigmas] for l in range(3)]
        face(y_ref, shift, field_y)

    @pl.when(step == 0)
    def _():
        side(0, xl_ref, yl_ref)

    @pl.when(step == 1)
    def _():
        side(1, xh_ref, yh_ref)
        low, high = xl_ref[0:X_ROWS, :], xh_ref[0:X_ROWS, :]
        px0_ref[...] = jnp.where(odd_x, low, high)
        px1_ref[...] = jnp.where(odd_x, high, low)
        low, high = yl_ref[...], yh_ref[...]
        py0_ref[...] = jnp.where(odd_y, low, high)
        py1_ref[...] = jnp.where(odd_y, high, low)


def edge_kernel(links_ref, ab_ref, rx0_ref, rx1_ref, ty0_ref, ty1_ref, tl_ref, th_ref):
    odd_x, odd_y = parity()

    def from_x(side, rows):
        first, second = rx0_ref[rows, :], rx1_ref[rows, :]
        return jnp.where(odd_x, first, second) if side == 0 else jnp.where(odd_x, second, first)

    for e, t_ref in enumerate((tl_ref, th_ref)):
        outer, inner = (0, 1) if e == 0 else (N - 1, N - 2)
        for side in range(2):
            link = link_of(links_ref, side)
            x = side * (N - 1)
            for fr, fi, k in pairs():
                layers = []
                for y in (outer, inner):
                    at = x * N + y
                    ab = (ab_ref[2 * k, at:at + 1, :], ab_ref[2 * k + 1, at:at + 1, :])
                    re = link * from_x(side, slice(fr * N + y, fr * N + y + 1))
                    im = link * from_x(side, slice(fi * N + y, fi * N + y + 1))
                    layers.append(times(ab, re, im))
                t_ref[side * NF + fr:side * NF + fr + 1, :] = trace(layers[0][0], layers[1][0])
                t_ref[side * NF + fi:side * NF + fi + 1, :] = trace(layers[0][1], layers[1][1])
            at = X_R + e * 24
            t_ref[24 + side * 24:48 + side * 24, :] = from_x(side, slice(at, at + 24))
    low, high = tl_ref[...], th_ref[...]
    ty0_ref[...] = jnp.where(odd_y, low, high)
    ty1_ref[...] = jnp.where(odd_y, high, low)


def solve_kernel(
    freq_ref, floor_ref, src_ref, adj_ref, sh_ref, sv_ref,
    u_ref, ab_ref, w_ref, *refs,
):
    scale = scale_of(freq_ref)
    odd_core = lax.rem(lax.axis_index("freq"), 2) == 1
    count = len(PIECES)
    keep_refs, send_refs, v_ref = refs[:count], refs[count:2 * count], refs[2 * count]
    zeros = jnp.zeros((PLANE, NZ), f32)
    for f in range(NF):
        for ref in (u_ref, v_ref):
            ref[f, 0:PLANE, :] = zeros
            ref[f, ROWS - PLANE:ROWS, :] = zeros

    def first_update(x, carry):
        there = pl.ds(pl.multiple_of(x * N, N), N)
        start = pl.multiple_of(base(x), 8)
        mask = mask_of(floor_column(floor_ref, x, 0, N))
        ab = []
        for k, ref in enumerate((sh_ref, sv_ref)):
            ab.append(factors(scale * ref[there, :] * mask))
            ab_ref[2 * k, there, :] = ab[k][0]
            ab_ref[2 * k + 1, there, :] = ab[k][1]
        zeros = jnp.zeros((8, NZ), f32)
        for fr, fi, k in pairs():
            ref, g = (src_ref, 0) if fr < 6 else (adj_ref, 6)
            re, im = times(ab[k], ref[fr - g, there, :], ref[fi - g, there, :])
            for f, value in ((fr, re), (fi, im)):
                u_ref[f, pl.ds(start, N), :] = value
                u_ref[f, pl.ds(start + N, 8), :] = zeros
                v_ref[f, pl.ds(start + N, 8), :] = zeros
        return carry

    lax.fori_loop(0, N, first_update, 0, unroll=4)

    def second_update(x, carry):
        there = pl.ds(pl.multiple_of(x * N, N), N)
        start = pl.multiple_of(base(x), 8)
        ab = [(ab_ref[2 * k, there, :], ab_ref[2 * k + 1, there, :]) for k in range(2)]
        for fr, fi, k in pairs():
            re, im = times(ab[k], stencil(u_ref, fr, x), stencil(u_ref, fi, x))
            v_ref[fr, pl.ds(start, N), :] = u_ref[fr, pl.ds(start, N), :] + re
            v_ref[fi, pl.ds(start, N), :] = u_ref[fi, pl.ds(start, N), :] + im
        return carry

    lax.fori_loop(0, N, second_update, 0, unroll=4)

    def last_update(x):
        there = pl.ds(pl.multiple_of(x * N, N), N)
        start = pl.multiple_of(base(x), 8)
        ab = [(ab_ref[2 * k, there, :], ab_ref[2 * k + 1, there, :]) for k in range(2)]
        term = [None, None]
        for comp in range(3):
            k = comp // 2
            new = []
            for solve in range(2):
                fr, fi = solve * 6 + comp, solve * 6 + 3 + comp
                re, im = times(ab[k], stencil(v_ref, fr, x), stencil(v_ref, fi, x))
                re = re + u_ref[fr, pl.ds(start, N), :]
                im = im + u_ref[fi, pl.ds(start, N), :]
                w_ref[fr, there, :] = re
                w_ref[fi, there, :] = im
                new.append((re, im))
            product = new[1][0] * new[0][1] + new[1][1] * new[0][0]
            term[k] = product if term[k] is None else term[k] + product
        return term

    for x in (0, 1, N - 2, N - 1):
        last_update(x)
    first = 2
    for size, keep_ref, send_ref in zip(PIECES, keep_refs, send_refs):
        def plane(j, carry, first=first, keep_ref=keep_ref, send_ref=send_ref):
            here = pl.ds(j * INNER, INNER)
            term = last_update(first + j)
            term_h, term_v = scale * term[0], scale * term[1]
            keep_ref[here, :] = pltpu.roll(jnp.where(odd_core, term_v, term_h), N - 2, 0)[0:INNER, :]
            send_ref[here, :] = pltpu.roll(jnp.where(odd_core, term_h, term_v), N - 2, 0)[0:INNER, :]
            return carry

        lax.fori_loop(0, size, plane, 0, unroll=4)
        first += size


def gather_kernel(ab_ref, w_ref, abr_ref, wr_ref):
    for at, y in enumerate((0, 1, N - 2, N - 1)):
        out = slice(at * N, (at + 1) * N)
        for k in range(4):
            abr_ref[k, out, :] = ab_ref[k, pl.ds(y, N, stride=N), :]
        for f in range(NF):
            wr_ref[f, out, :] = w_ref[f, pl.ds(y, N, stride=N), :]


def boundary_kernel(
    freq_ref, links_ref, u_ref, ab_ref, w_ref, abr_ref, wr_ref, py0_ref, py1_ref,
    rx0_ref, rx1_ref, ry0_ref, ry1_ref, rt0_ref, rt1_ref, keep_in_ref, send_in_ref,
    planes_ref, rows_ref, keep_ref, send_ref,
):
    scale = scale_of(freq_ref)
    odd_x, odd_y = parity()
    odd_core = lax.rem(lax.axis_index("freq"), 2) == 1
    link = [link_of(links_ref, k) for k in range(4)]
    row = lax.broadcasted_iota(jnp.int32, (N, NZ), 0)

    def pick(odd, side, first_ref, second_ref, rows):
        first, second = first_ref[rows, :], second_ref[rows, :]
        return jnp.where(odd, first, second) if side == 0 else jnp.where(odd, second, first)

    def from_x(side, at, size):
        return pick(odd_x, side, rx0_ref, rx1_ref, slice(at, at + size))

    def from_y(side, at, size):
        return pick(odd_y, side, ry0_ref, ry1_ref, slice(at, at + size))

    def from_t(side, at, size):
        return pick(odd_y, side, rt0_ref, rt1_ref, slice(at, at + size))

    def ends(first, last):
        return jnp.where(row == 0, first, jnp.where(row == N - 1, last, 0.0))

    def ab_plane(k, x):
        return ab_ref[2 * k, x * N:(x + 1) * N, :], ab_ref[2 * k + 1, x * N:(x + 1) * N, :]

    def ab_row(k, at):
        return abr_ref[2 * k, at * N:(at + 1) * N, :], abr_ref[2 * k + 1, at * N:(at + 1) * N, :]

    near_x = [[factors(from_x(s, X_S + k * N, N)) for k in range(2)] for s in range(2)]
    near_y = [[factors(from_y(s, X_S + k * N, N)) for k in range(2)] for s in range(2)]
    corner = [[[[factors(from_x(s, X_C + e * 4 + k * 2 + layer, 1)) for layer in range(2)]
                for k in range(2)] for e in range(2)] for s in range(2)]

    row_factors = [[[ab_row(k, at) for at in ats] for ats in ((0, 1), (3, 2))] for k in range(2)]

    for fr, fi, k in pairs():
        both = (fr, fi)
        edge, ghost_y = [], []
        for e in range(2):
            g1 = [link[2 + e] * from_y(e, f * N, N) for f in both]
            edge.append((g1, times(row_factors[k][e][0], *g1)))
            own = [pick(odd_y, e, py0_ref, py1_ref, slice(f * N, (f + 1) * N)) for f in both]
            back = times(near_y[e][k], *own)
            ghost_y.append([
                link[2 + e] * (from_y(e, FACE + f * N, N) + KEEP * back[c] + ends(from_t(e, f, 1), from_t(e, NF + f, 1)))
                for c, f in enumerate(both)
            ])
        for s in range(2):
            x0, x1, x2 = (0, 1, 2) if s == 0 else (N - 1, N - 2, N - 3)
            g1 = [link[s] * from_x(s, f * N, N) + ends(edge[0][0][c][x0:x0 + 1, :], edge[1][0][c][x0:x0 + 1, :])
                  for c, f in enumerate(both)]
            ab0, ab1 = ab_plane(k, x0), ab_plane(k, x1)
            w0 = times(ab0, *g1)
            own = [trace(u_ref[f, base(x0):base(x0) + N, :], u_ref[f, base(x1):base(x1) + N, :]) for f in both]
            back = times(near_x[s][k], *own)
            corners = []
            for e in range(2):
                layers = []
                for layer in range(2):
                    relay = [from_t(e, 24 + s * 24 + f * 2 + layer, 1) for f in both]
                    layers.append(times(corner[s][e][k][layer], *relay))
                corners.append([trace(layers[0][c], layers[1][c]) for c in range(2)])
            rhs0, rhs1 = [], []
            for c, f in enumerate(both):
                ghost = link[s] * (from_x(s, FACE + f * N, N) + KEEP * back[c] + ends(corners[0][c], corners[1][c]))
                m1 = ends(edge[0][1][c][x1:x1 + 1, :], edge[1][1][c][x1:x1 + 1, :])
                m2 = ends(edge[0][1][c][x2:x2 + 1, :], edge[1][1][c][x2:x2 + 1, :])
                side0 = ends(ghost_y[0][c][x0:x0 + 1, :], ghost_y[1][c][x0:x0 + 1, :])
                side1 = ends(ghost_y[0][c][x1:x1 + 1, :], ghost_y[1][c][x1:x1 + 1, :])
                rhs0.append(row_neighbours(w0[c]) + lane_neighbours(w0[c]) + m1 + ghost + side0)
                rhs1.append(w0[c] + m2 + row_neighbours(m1) + lane_neighbours(m1) + side1)
            fix0, fix1 = times(ab0, *rhs0), times(ab1, *rhs1)
            at0, at1 = (0, 1) if s == 0 else (3, 2)
            for c, f in enumerate(both):
                planes_ref[f, at0 * N:(at0 + 1) * N, :] = w_ref[f, x0 * N:(x0 + 1) * N, :] + fix0[c]
                planes_ref[f, at1 * N:(at1 + 1) * N, :] = w_ref[f, x1 * N:(x1 + 1) * N, :] + fix1[c]
        for e in range(2):
            w0 = edge[e][1]
            rhs = [row_neighbours(w0[c]) + lane_neighbours(w0[c]) + ghost_y[e][c] for c in range(2)]
            fix0 = times(row_factors[k][e][0], *rhs)
            fix1 = times(row_factors[k][e][1], *w0)
            at0, at1 = (0, 1) if e == 0 else (3, 2)
            for c, f in enumerate(both):
                rows_ref[f, at0 * N:(at0 + 1) * N, :] = wr_ref[f, at0 * N:(at0 + 1) * N, :] + fix0[c]
                rows_ref[f, at1 * N:(at1 + 1) * N, :] = wr_ref[f, at1 * N:(at1 + 1) * N, :] + fix1[c]
    keep_ref[8 * N:, :] = keep_in_ref[...]
    send_ref[8 * N:, :] = send_in_ref[...]
    for ref, at in ((planes_ref, 0), (rows_ref, 4 * N)):
        term = [None, None]
        for comp in range(3):
            product = ref[6 + comp] * ref[3 + comp] + ref[9 + comp] * ref[comp]
            term[comp // 2] = product if comp % 2 == 0 else term[0] + product
        term_h, term_v = scale * term[0], scale * term[1]
        keep_ref[at:at + 4 * N, :] = jnp.where(odd_core, term_v, term_h)
        send_ref[at:at + 4 * N, :] = jnp.where(odd_core, term_h, term_v)


def put_boundary(step, block_ref, index, planes, rows, size=STEP):
    for at, y in enumerate((0, 1, N - 2, N - 1)):
        block_ref[(*index, pl.ds(y, size, stride=N), slice(None))] = rows(at)

    @pl.when(step == 0)
    def _():
        block_ref[(*index, slice(0, 2 * N), slice(None))] = planes(0)

    @pl.when(step == N // size - 1)
    def _():
        block_ref[(*index, slice((size - 2) * N, size * N), slice(None))] = planes(2 * N)


def field_kernel(w_ref, planes_ref, rows_ref, out_ref):
    step = pl.program_id(0)
    out_ref[...] = w_ref[0:6, pl.ds(pl.multiple_of(step * BLOCK, BLOCK), BLOCK), :]
    for f in range(6):
        put_boundary(
            step, out_ref, (f,),
            lambda at, f=f: planes_ref[f, at:at + 2 * N, :],
            lambda at, f=f: rows_ref[f, pl.ds(pl.multiple_of(at * N + step * STEP, 8), STEP), :],
        )


def gradient_kernel(mine_ref, other_ref, mine_b_ref, other_b_ref, ab_ref, sh_ref, sv_ref, gh_ref, gv_ref, total_ref):
    step = pl.program_id(0)
    odd_core = lax.rem(lax.axis_index("freq"), 2) == 1
    block = pl.ds(pl.multiple_of(step * LAST * N, LAST * N), LAST * N)
    mask = (ab_ref[0, block, :] > 0.0).astype(f32)
    for k, (sigma_ref, out_ref) in enumerate(((sh_ref, gh_ref), (sv_ref, gv_ref))):
        first = odd_core if k == 1 else jnp.logical_not(odd_core)
        for j in range(LAST):
            inner = jnp.clip(step * LAST + j - 2, 0, PIECES[0] - 1)
            rows = pl.ds(inner * INNER, INNER)
            total_ref[j * N + 2:(j + 1) * N - 2, :] = jnp.where(first, mine_ref[rows, :], other_ref[rows, :])

        def boundary(rows):
            return jnp.where(first, mine_b_ref[rows, :], other_b_ref[rows, :])

        @pl.when(step == N // LAST - 1)
        def _():
            for p in range(PIECES[1]):
                at, rows = (LAST - 2 - PIECES[1] + p) * N + 2, 8 * N + p * INNER
                total_ref[at:at + INNER, :] = boundary(slice(rows, rows + INNER))

        put_boundary(
            step, total_ref, (),
            lambda at: boundary(slice(at, at + 2 * N)),
            lambda at: boundary(pl.ds(pl.multiple_of((4 + at) * N + step * LAST, 8), LAST)),
            LAST,
        )
        out_ref[...] = sigma_ref[block, :] * mask * total_ref[...]


def swap_pairs(axis, odd):
    pairs_of = []
    for i in range(SUBS):
        at = [i % SX, i // SX]
        at[axis] += 1 if at[axis] % 2 == odd else -1
        if 0 <= at[axis] < SX:
            pairs_of.append((i, at[1] * SX + at[0]))
    return pairs_of


def swap(value, axis, odd):
    return lax.ppermute(value, "sub", swap_pairs(axis, odd))


def swap_freq(value, flip):
    return lax.ppermute(value, "freq", [(i, i ^ flip) for i in range(4)])


def sds(*shape):
    return jax.ShapeDtypeStruct(shape, f32)


def on_device(source, adjoint_source, sigma_h, sigma_v, seafloor, links, freq_index):
    steps = N // STEP
    src = in_hbm(source.reshape(6, N, N, NZ))
    adj = in_hbm(adjoint_source.reshape(6, N, N, NZ))
    cond_h = sigma_h.reshape(CELLS, NZ)
    cond_v = sigma_v.reshape(CELLS, NZ)
    cond_h4 = in_hbm(sigma_h.reshape(N, N, NZ))
    cond_v4 = in_hbm(sigma_v.reshape(N, N, NZ))
    floor = in_hbm(seafloor.reshape(N, N))
    links = in_hbm(links)
    smem = whole(pltpu.SMEM)

    def block3(size):
        return pl.BlockSpec((size, BLOCK, NZ), lambda i: (0, jnp.minimum(i, steps - 1), 0))

    block2 = pl.BlockSpec((BLOCK, NZ), lambda i: (jnp.minimum(i, steps - 1), 0))

    flat_src, flat_adj = in_hbm(source.reshape(6, CELLS, NZ)), in_hbm(adjoint_source.reshape(6, CELLS, NZ))
    flat_h, flat_v = in_hbm(cond_h), in_hbm(cond_v)
    last = N // 4 - 1
    field_x = pl.BlockSpec((6, 4 * N, NZ), lambda i: (0, i * last, 0))
    sigma_x = pl.BlockSpec((4 * N, NZ), lambda i: (i * last, 0))
    field_y = pl.BlockSpec((6, N, 8, NZ), lambda i: (0, 0, i * (N // 8 - 1), 0))
    sigma_y = pl.BlockSpec((N, 8, NZ), lambda i: (0, i * (N // 8 - 1), 0))
    px0, px1, py0, py1 = pl.pallas_call(
        strip_kernel,
        grid=(2,),
        in_specs=[smem] + [whole()] * 2 + [field_x, field_x, sigma_x, sigma_x, field_y, field_y, sigma_y, sigma_y],
        out_specs=[whole()] * 4,
        out_shape=[sds(X_ROWS, NZ), sds(X_ROWS, NZ), sds(Y_ROWS, NZ), sds(Y_ROWS, NZ)],
        scratch_shapes=[pltpu.VMEM((X_ROWS + 8, NZ), f32)] * 2 + [pltpu.VMEM((Y_ROWS, NZ), f32)] * 2,
        compiler_params=params(14),
        cost_estimate=cost(10**6, 12 * 2**20),
        name="strips",
    )(freq_index, links, floor, flat_src, flat_adj, flat_h, flat_v, src, adj, cond_h4, cond_v4)
    ry1 = swap(py1, 1, 1)
    ry0 = swap(py0, 1, 0)
    rx1 = swap(px1, 0, 1)
    rx0 = swap(px0, 0, 0)

    u, ab, w, *terms = pl.pallas_call(
        solve_kernel,
        in_specs=[smem] + [whole()] * 5,
        out_specs=[whole()] * (3 + 2 * len(PIECES)),
        out_shape=[
            pltpu.VMEM((NF, ROWS, NZ), f32), pltpu.VMEM((4, CELLS, NZ), f32), pltpu.VMEM((NF, CELLS, NZ), f32),
        ] + [sds(size, NZ) for size in PIECE_ROWS] * 2,
        scratch_shapes=[pltpu.VMEM((NF, ROWS, NZ), f32)],
        compiler_params=params(24),
        cost_estimate=cost(60 * NF * CELLS * NZ, 40 * 2**20),
        name="solve",
    )(
        freq_index, floor, source.reshape(6, CELLS, NZ), adjoint_source.reshape(6, CELLS, NZ), cond_h, cond_v
    )

    ty0, ty1 = pl.pallas_call(
        edge_kernel,
        in_specs=[whole()] * 4,
        out_specs=[whole()] * 2,
        out_shape=[sds(T_ROWS, NZ)] * 2,
        scratch_shapes=[pltpu.VMEM((T_ROWS, NZ), f32)] * 2,
        compiler_params=params(4),
        cost_estimate=cost(1000, 1000),
        name="edges",
    )(links, ab, rx0, rx1)
    rt1 = swap(ty1, 1, 1)
    rt0 = swap(ty0, 1, 0)

    mine = terms[0] + swap_freq(terms[2], 1)
    partner = swap_freq(mine, 2)

    abr, wr = pl.pallas_call(
        gather_kernel,
        in_specs=[whole()] * 2,
        out_specs=[whole()] * 2,
        out_shape=[pltpu.VMEM((4, 4 * N, NZ), f32), pltpu.VMEM((NF, 4 * N, NZ), f32)],
        compiler_params=params(4),
        cost_estimate=cost(1000, 1000),
        name="gather",
    )(ab, w)
    planes, rows, keep_b, send_b = pl.pallas_call(
        boundary_kernel,
        in_specs=[smem] + [whole()] * 16,
        out_specs=[whole()] * 4,
        out_shape=[pltpu.VMEM((NF, 4 * N, NZ), f32)] * 2 + [sds(8 * N + PIECE_ROWS[1], NZ)] * 2,
        compiler_params=params(8),
        cost_estimate=cost(1000, 1000),
        name="boundary",
    )(freq_index, links, u, ab, w, abr, wr, py0, py1, rx0, rx1, ry0, ry1, rt0, rt1, terms[1], terms[3])

    forward = pl.pallas_call(
        field_kernel,
        grid=(steps,),
        in_specs=[whole()] * 3,
        out_specs=block3(6),
        out_shape=sds(6, CELLS, NZ),
        compiler_params=params(6),
        cost_estimate=cost(1000, 1000),
        name="field",
    )(w, planes, rows)

    mine_b = keep_b + swap_freq(send_b, 1)
    partner_b, partner, forward = lax.optimization_barrier((swap_freq(mine_b, 2), partner, forward))
    mine = mine + partner
    mine_b = mine_b + partner_b
    other = swap_freq(mine, 1)
    other_b = swap_freq(mine_b, 1)

    grad_h, grad_v = pl.pallas_call(
        gradient_kernel,
        grid=(N // LAST,),
        in_specs=[whole()] * 7,
        out_specs=[pl.BlockSpec((LAST * N, NZ), lambda i: (i, 0))] * 2,
        out_shape=[sds(CELLS, NZ)] * 2,
        scratch_shapes=[pltpu.VMEM((LAST * N, NZ), f32)],
        compiler_params=params(6),
        cost_estimate=cost(1000, 1000),
        name="gradient",
    )(mine, other, mine_b, other_b, ab, cond_h, cond_v)

    return (
        forward.reshape(1, 1, 2, 3, N, N, NZ),
        grad_h.reshape(1, N, N, NZ),
        grad_v.reshape(1, N, N, NZ),
    )


def solution(mesh):
    return jax.shard_map(
        on_device,
        mesh=mesh,
        in_specs=(
            P("sub", None, None, None, None, None),
            P("freq", "sub", None, None, None, None, None),
            P("sub", None, None, None),
            P("sub", None, None, None),
            P("sub", None, None),
            P("sub", None),
            P("freq"),
        ),
        out_specs=(
            P("freq", "sub", None, None, None, None, None),
            P("sub", None, None, None),
            P("sub", None, None, None),
        ),
        check_vma=False,
    )
```
